256 devices in a mesh: dp: 128 (over x, y, z), group: 2 (over core).
Axes of the slice: x: 4, y: 4, z: 8, core: 2. Of those that a mesh axis runs over, the one named last changes fastest.
Arguments:
- tokens_in: bfloat16 [128, 256, 1536], P('dp', None, 'group'), may hold values from -24 to 24
- dw_kernel: float32 [7, 1536], P(None, 'group'), may hold values from -2 to 2
- point_weight: bfloat16 [1536, 1536], P(None, 'group'), may hold values from -0.15625 to 0.15625
- positive_emb: bfloat16 [128, 1536], P('dp', 'group'), may hold values from -0.15625 to 0.15625
- bank: bfloat16 [16384, 1536], P('dp', 'group'), may hold values from -0.15625 to 0.15625
- neg_owner: int32 [16384, 1], P('dp'), may hold values from 0 to 127; in each aligned block of 128 rows (0 to 127, 128 to 255, ...) at most 2 rows name the same one
- neg_block: int32 [16384], P('dp'), may hold values from 0 to 15
Outputs:
- grad_bank: float32 [16384, 1536], P('dp', 'group')
- grad_kernel: float32 [7, 1536], P(None, 'group')
- grad_weight: float32 [1536, 1536], P('dp', 'group')
The draws below stay inside these ranges and needn't reach their ends.
Inputs may be any that keep to these rules, and one draw needn't show every extreme that they name: `neg_owner`: among the 128 requests of one batch shard (aligned blocks of 128 rows), no owner is named more than 2 times.
All inputs are finite; a program needn't handle non-finite values.
Results may differ from the reference program's by a relative error of at most 0.0036.
Values may be sent and summed in bfloat16 or wider, within the bound.
No kernel may reach another device: no remote copies, remote signals or barrier semaphores. Data moves between devices by JAX's collectives and lax.ppermute only.
A program may use at most 128 MiB of HBM per device.

```python
import math
import jax
import jax.numpy as jnp
import numpy as np
from jax import lax

C = 1536
KW = 7
LEN = 256
SEQ_DEV = 1
ROWS = 8
OWN_BLK = 16
CAP = 2
NEG = 128
SEQS = 128
BANK = 16384
N_DP = 128


def with_ends(values, stream_key, smallest, high):
    spot = [jax.random.randint(jax.random.fold_in(stream_key, axis), (), 0, length) for axis, length in enumerate(values.shape)]
    widest = values.shape.index(max(values.shape))
    next_to = spot[:widest] + [(spot[widest] + 1) % values.shape[widest]] + spot[widest + 1:]
    return values.at[tuple(spot)].set(smallest).at[tuple(next_to)].set(high)


def strengthened(drawn, rng, source, target, parts, factor):
    owner, partner = [(jnp.arange(drawn.shape[axis_at]) // (drawn.shape[axis_at] // parts)).reshape([-1 if axis == axis_at else 1 for axis in range(drawn.ndim)]) for axis_at in (source, target)]
    chosen = jax.random.permutation(rng, parts)[partner]
    strong = (owner == chosen) | (owner == (partner + parts // 2) % parts)
    return jnp.where(strong, factor * drawn, drawn)


def steps_of(key, dims, shards, least, high):
    level = 1.0
    for dim, parts in shards:
        heights = jax.random.uniform(jax.random.fold_in(jax.random.fold_in(key, 6), dim), (parts,), jnp.float32, least / len(shards), high / len(shards))
        level = level * jnp.repeat(jnp.exp(heights), dims[dim] // parts).reshape((-1,) + (1,) * (len(dims) - 1 - dim))
    return level


def routed_block(key, own, number, rows, count, top, limit, slope):
    ranking = jax.random.permutation(key, count)
    heavy_load, ordinary = shares(count, rows * top, limit, slope, True), shares(count, rows * top, limit, slope, False)
    places = jnp.arange(count)

    def named(tallies, turn):
        used = int((tallies > 0).sum())
        fixed = max(1, used // 4)
        shifted = fixed + (places - fixed + turn * (used - fixed)) % max(1, count - fixed)
        return jnp.zeros((count,), jnp.int32).at[ranking[jnp.where(places < fixed, places, shifted)]].set(jnp.asarray(tallies, jnp.int32))

    tallies = jnp.where(number % 4 == 0, named(heavy_load, number // 4), named(ordinary, number - number // 4 - 1))
    mixed = jax.random.permutation(jax.random.fold_in(own, 3), count)
    source_of, taker = mixed[0:count // 2 * 2:2], mixed[1:count // 2 * 2:2]
    slack = jnp.minimum(tallies[source_of] - 1, limit - tallies[taker]) // 2
    slack = jnp.where((source_of == ranking[0]) | (taker == ranking[0]) | (tallies[taker] == 0), 0, jnp.maximum(slack, 0))
    shifted = jax.random.randint(jax.random.fold_in(own, 4), (count // 2,), 0, 1 << 20) % (slack + 1)
    tallies = tallies.at[source_of].add(-shifted).at[taker].add(shifted)
    labels = jnp.searchsorted(jnp.cumsum(tallies), jnp.arange(rows * top), side="right").astype(jnp.int32)
    listing = labels.reshape(top, rows).T
    listing = listing[jax.random.permutation(jax.random.fold_in(own, 1), rows)]
    turn = jax.random.randint(jax.random.fold_in(own, 2), (rows, 1), 0, top)
    return jnp.take_along_axis(listing, (jnp.arange(top)[None, :] + turn) % top, axis=1)


def shares(amount, total, reach, slope, full):
    weights = [(1 << 20) // math.isqrt(rank ** slope) + 1 for rank in range(1, amount + 1)]
    largest = reach if full else min(reach, max(-(-total // amount), total * weights[0] // sum(weights)))
    least = 1 if total - largest >= amount - 1 else 0
    given, rest = [largest] + [least] * (amount - 1), total - largest - least * (amount - 1)
    while rest > 0:
        movable = [i for i in range(1, amount) if given[i] < largest] or [i for i in range(1, amount) if given[i] < reach]
        mass, remaining = sum([weights[i] for i in movable]), rest
        for i in movable:
            addition = min(reach - given[i], max(1, remaining * weights[i] // mass), rest)
            given[i] = given[i] + addition
            rest = rest - addition
    return np.array(given)


def normal_values(key, shape, width, limit, cuts=(), kind=jnp.bfloat16):
    loudness = steps_of(key, shape, cuts, -0.22, 0.18) if cuts else 1.0
    drawn = jax.random.normal(key, shape, jnp.float32) * width * loudness
    return jnp.minimum(jnp.maximum(drawn, -limit), limit).astype(kind)


def heavy_noise(rng, dims, deviation, bound, cuts, heavy, held_as=jnp.bfloat16):
    entries = deviation * jax.random.normal(rng, dims, jnp.float32)
    if cuts:
        entries = entries * steps_of(rng, dims, cuts, -0.22, 0.18)
    return jnp.clip(strengthened(entries, jax.random.fold_in(rng, 3), *heavy), -bound, bound).astype(held_as)


def setup_inputs(seed: int = 0) -> dict:
    key_list = jax.random.split(jax.random.key(seed), 8)
    tokens_in = heavy_noise(key_list[0], (SEQS, LEN, C), 1.0, 24.0, ((0, 128), (2, 2)), (0, 2, 128, 5.5))
    dw_kernel = normal_values(key_list[1], (KW, C), KW ** -0.5, 2.0, ((1, 2),), jnp.float32)
    point_weight = normal_values(key_list[2], (C, C), C ** -0.5, 0.15625, ((1, 2),))
    positive_emb = normal_values(key_list[3], (SEQS, C), C ** -0.5, 0.15625, ((0, 128), (1, 2)))
    bank = normal_values(key_list[4], (BANK, C), C ** -0.5, 0.15625, ((0, 128), (1, 2)))
    neg_owner_keys = jax.random.split(jax.random.fold_in(key_list[5], 1), (N_DP * NEG) // NEG)
    neg_owner_turns = jax.random.permutation(jax.random.fold_in(key_list[5], 3), (N_DP * NEG) // NEG)
    neg_owner = jax.vmap(lambda own, number: routed_block(jax.random.fold_in(key_list[5], 2), own, number, NEG, N_DP, 1, CAP, 2))(neg_owner_keys, neg_owner_turns).reshape((N_DP * NEG, 1))
    neg_block = with_ends(jax.random.randint(key_list[6], (N_DP * NEG,), 0, OWN_BLK), jax.random.fold_in(key_list[6], 1), 0, OWN_BLK - 1).astype(jnp.int32)
    return dict(tokens_in=tokens_in, dw_kernel=dw_kernel, point_weight=point_weight, positive_emb=positive_emb, bank=bank, neg_owner=neg_owner, neg_block=neg_block)


SOFTMAX_TEMPER = 0.07
LOSS_SCALE = 256.0
EPSILON = 1e-06
PRECISE = lax.Precision.HIGHEST

def depthwise(tokens, kernel):
    margin = kernel.shape[0] // 2
    seq_length = tokens.shape[1]
    padded = jnp.pad(tokens.astype(jnp.float32), ((0, 0), (margin, margin), (0, 0)))
    running_sum = jnp.zeros(tokens.shape, jnp.float32)
    for tap_index in range(kernel.shape[0]):
        running_sum = running_sum + kernel[tap_index] * padded[:, tap_index:tap_index + seq_length, :]
    return (running_sum, padded)

def kernel_term(grad_hidden, padded, tap_count):
    seq_length = grad_hidden.shape[1]
    return jnp.stack([lax.optimization_barrier(jnp.sum(grad_hidden * padded[:, tap_index:tap_index + seq_length, :], axis=(0, 1))) for tap_index in range(tap_count)])

def gelu_back(mixed_out, cotangent):
    return jax.vjp(lambda entry_value: jax.nn.gelu(entry_value, approximate=True), mixed_out)[1](cotangent)[0]

def reference(tokens_in, dw_kernel, point_weight, positive_emb, bank, neg_owner, neg_block):
    own_rows = OWN_BLK * ROWS
    column_count = SEQ_DEV + own_rows + NEG * ROWS
    full_width = point_weight.shape[0]
    offsets = jnp.arange(ROWS, dtype=jnp.int32)
    target = jnp.eye(SEQ_DEV, column_count, dtype=jnp.float32)

    def one_shard(running, shard_index):
        bank_grad, weight_grad, kernel_grad = running
        tokens = lax.dynamic_slice_in_dim(tokens_in, shard_index * SEQ_DEV, SEQ_DEV, 0)
        positives = lax.dynamic_slice_in_dim(positive_emb, shard_index * SEQ_DEV, SEQ_DEV, 0)
        local_start = (shard_index * own_rows).astype(jnp.int32)
        local_keys = lax.dynamic_slice_in_dim(bank, local_start, own_rows, 0)
        owners = lax.dynamic_slice_in_dim(neg_owner[:, 0], shard_index * NEG, NEG, 0)
        blocks = lax.dynamic_slice_in_dim(neg_block, shard_index * NEG, NEG, 0)
        neg_index = ((owners * own_rows + blocks * ROWS)[:, None] + offsets[None, :]).reshape(-1).astype(jnp.int32)
        negatives = jnp.take(bank, neg_index, axis=0)
        key_rows = jnp.concatenate([positives, local_keys, negatives], axis=0)
        hidden_f, padded = depthwise(tokens, dw_kernel)
        hidden = hidden_f.astype(jnp.bfloat16).reshape(SEQ_DEV * LEN, full_width)
        mixed_out = lax.dot_general(hidden, point_weight, (((1,), (1,)), ((), ())), preferred_element_type=jnp.float32)
        activated = jax.nn.gelu(mixed_out, approximate=True)
        embedding = lax.optimization_barrier(jnp.mean(tokens.astype(jnp.float32) + activated.reshape(SEQ_DEV, LEN, full_width), axis=1))
        key_float = key_rows.astype(jnp.float32)
        inner_products = lax.dot_general(embedding, key_float, (((1,), (1,)), ((), ())), precision=PRECISE)
        embedding_norm = jnp.sqrt(lax.optimization_barrier(jnp.sum(embedding * embedding, axis=1)) + EPSILON)
        key_length_norm = jnp.sqrt(lax.optimization_barrier(jnp.sum(key_float * key_float, axis=1)) + EPSILON)
        score_matrix = inner_products / (SOFTMAX_TEMPER * embedding_norm[:, None] * key_length_norm[None, :])
        exponent = jnp.exp(score_matrix)
        weights = exponent / lax.optimization_barrier(jnp.sum(exponent, axis=1, keepdims=True))
        score_gradient = LOSS_SCALE * (weights - target)
        blend_factor = score_gradient / (SOFTMAX_TEMPER * key_length_norm[None, :])
        unit_query = embedding / embedding_norm[:, None]
        row_weight = lax.optimization_barrier(jnp.sum(score_gradient * score_matrix, axis=1))
        column_weight = lax.optimization_barrier(jnp.sum(score_gradient * score_matrix, axis=0))
        key_scale = column_weight / (key_length_norm * key_length_norm)
        query_dir = jnp.dot(blend_factor, key_float, precision=PRECISE)
        embed_grad = (query_dir - row_weight[:, None] * unit_query) / embedding_norm[:, None]
        key_grad = lax.dot_general(blend_factor, unit_query, (((0,), (0,)), ((), ())), precision=PRECISE) - key_scale[:, None] * key_float
        local_index = (local_start + jnp.arange(own_rows, dtype=jnp.int32)).astype(jnp.int32)
        all_index = jnp.concatenate([local_index, neg_index], axis=0)
        bank_grad = bank_grad.at[all_index].add(key_grad[SEQ_DEV:])
        act_grad = jnp.broadcast_to((embed_grad / LEN)[:, None, :], (SEQ_DEV, LEN, full_width)).reshape(SEQ_DEV * LEN, full_width)
        mixed_grad = gelu_back(mixed_out, act_grad).astype(jnp.bfloat16)
        hidden_grad = jnp.dot(mixed_grad, point_weight, preferred_element_type=jnp.float32)
        weight_grad = weight_grad + lax.dot_general(mixed_grad, hidden, (((0,), (0,)), ((), ())), preferred_element_type=jnp.float32)
        kernel_grad = kernel_grad + kernel_term(hidden_grad.reshape(SEQ_DEV, LEN, full_width), padded, KW)
        return ((bank_grad, weight_grad, kernel_grad), None)
    start_state = (jnp.zeros(bank.shape, jnp.float32), jnp.zeros((full_width, full_width), jnp.float32), jnp.zeros((KW, full_width), jnp.float32))
    final_state, unused = lax.scan(one_shard, start_state, jnp.arange(N_DP, dtype=jnp.int32))
    bank_grad, weight_grad, kernel_grad = final_state
    return (bank_grad, kernel_grad / N_DP, weight_grad / N_DP)
```

```python
import jax
import jax.numpy as jnp
from jax import lax
from jax.experimental import pallas as pl
from jax.experimental.pallas import tpu as pltpu
from jax.sharding import Mesh, PartitionSpec as P

KW = 7
LEN = 256
HALF = 768
N_DP = 128
NX, NY, NZ = 4, 4, 8
PLANE = NX * NY
ROWS = 8
OWN = 128
OUT_ROWS = 12
Z_ROWS = OUT_ROWS * NZ
PACK = 16
EXTRA = 128
WIDE = HALF + EXTRA
LANES = 128
COLS = HALF // LANES

TEMPER = 0.07
SCALE = 256.0
EPSILON = 1e-06
GELU_C = 0.7978845608028654
GELU_A = 0.044715
PRECISE = lax.Precision.HIGHEST
F32 = jnp.float32
BF16 = jnp.bfloat16

DP = ("x", "y", "z")
SWAP = [(0, 1), (1, 0)]
VMEM_BYTES = 50 * 2**20

NT = (((1,), (1,)), ((), ()))
NN = (((1,), (0,)), ((), ()))
TN = (((0,), (0,)), ((), ()))


def dot(a, b, dims, precision=None):
    return lax.dot_general(a, b, dims, precision=precision, preferred_element_type=F32)


def call(body, outs, name, scratch=(), scalars=0, n_in=0, flops=0):
    smem = [pl.BlockSpec(memory_space=pltpu.SMEM)] * scalars
    vmem = [pl.BlockSpec(memory_space=pltpu.VMEM)] * n_in
    return pl.pallas_call(
        body,
        out_shape=[jax.ShapeDtypeStruct(s, d) for s, d in outs],
        in_specs=smem + vmem,
        out_specs=[pl.BlockSpec(memory_space=pltpu.VMEM)] * len(outs),
        scratch_shapes=list(scratch),
        compiler_params=pltpu.CompilerParams(vmem_limit_bytes=VMEM_BYTES),
        cost_estimate=pl.CostEstimate(flops=flops, bytes_accessed=1 << 20, transcendentals=0),
        name=name,
    )


def fill_padded(tokens_ref, pad):
    pad[0:8, :] = jnp.zeros((8, HALF), F32)
    pad[LEN + 8 : LEN + 16, :] = jnp.zeros((8, HALF), F32)
    for t in range(0, LEN, 32):
        pad[8 + t : 40 + t, :] = tokens_ref[t : t + 32, :].astype(F32)


def conv_body(place, tokens_ref, dw_ref, w_ref, hidden_ref, other_ref, pad):
    fill_padded(tokens_ref, pad)
    for t in range(0, LEN, 32):
        total = jnp.zeros((32, HALF), F32)
        for k in range(KW):
            total = total + dw_ref[k : k + 1, :] * pad[5 + k + t : 37 + k + t, :]
        hidden_ref[t : t + 32, :] = total.astype(BF16)
    start = pl.multiple_of((1 - place[0]) * HALF, HALF)
    other_ref[...] = dot(hidden_ref[...], w_ref[pl.ds(start, HALF), :], NT)


def own_body(place, hidden_ref, w_ref, owner_ref, block_ref, own_ref, table_ref):
    start = pl.multiple_of(place[0] * HALF, HALF)
    own_ref[...] = dot(hidden_ref[...], w_ref[pl.ds(start, HALF), :], NT)
    lane = lax.broadcasted_iota(jnp.int32, (OWN, LANES), 1)
    named = (owner_ref[...] == lane).astype(F32)
    blocks = jnp.broadcast_to(block_ref[...].astype(F32), (LANES, OWN)).T
    wanted = (blocks == lane.astype(F32)).astype(F32)
    table_ref[...] = dot(named.T.astype(BF16), wanted.astype(BF16), NN)


def embed_body(own_ref, other_ref, tokens_ref, table_ref, slope_ref, emb_ref, send_ref):
    total = jnp.zeros((8, HALF), F32)
    for t in range(0, LEN, 32):
        x = own_ref[t : t + 32, :] + other_ref[t : t + 32, :]
        sq = x * x
        th = jnp.tanh(GELU_C * x * (1.0 + GELU_A * sq))
        half = 0.5 * (1.0 + th)
        slope_ref[t : t + 32, :] = half + (0.5 * GELU_C) * x * (1.0 - th * th) * (
            1.0 + (3.0 * GELU_A) * sq
        )
        y = tokens_ref[t : t + 32, :].astype(F32) + x * half
        total = total + (y[0:8] + y[8:16]) + (y[16:24] + y[24:32])
    emb = jnp.sum(total, axis=0, keepdims=True) * (1.0 / LEN)
    emb_ref[...] = jnp.broadcast_to(emb, (8, HALF))
    send_ref[:, 0, 0:HALF] = jnp.broadcast_to(emb, (N_DP, HALF))
    send_ref[:, 0, HALF:WIDE] = table_ref[...]


def dots_body(recv_ref, bank_ref, emb_ref, pos_ref, packet_ref):
    e = recv_ref[:, 0, 0:HALF]
    key = bank_ref[...].astype(F32)
    packet_ref[0:OWN, :] = dot(key, e, NT, PRECISE)
    ones = jnp.ones((8, HALF), F32)
    packet_ref[OWN : OWN + 8, :] = dot(ones, e * e, NT, PRECISE)
    ksq = jnp.sum(key * key, axis=1, keepdims=True)
    packet_ref[OWN + 8 : 2 * OWN + 8, :] = jnp.broadcast_to(ksq, (OWN, LANES))
    emb = emb_ref[0:1, :]
    pos = pos_ref[...].astype(F32)
    rows = (emb * emb, emb * pos, pos * pos)
    for i in range(3):
        value = jnp.sum(rows[i], axis=1, keepdims=True)
        packet_ref[2 * OWN + 8 + 8 * i : 2 * OWN + 16 + 8 * i, :] = jnp.broadcast_to(
            value, (8, LANES)
        )


PACKET = 2 * OWN + 32


def scores_body(
    place, mine_ref, theirs_ref, recv_ref, bank_ref, send_ref, coef_ref, kcoef_ref, scal_ref
):
    full = mine_ref[...] + theirs_ref[...]
    en = jnp.sqrt(full[OWN : OWN + 1] + EPSILON)
    kn = jnp.sqrt(full[OWN + 8 : 2 * OWN + 8] + EPSILON)
    scal_ref[...] = full[2 * OWN + 8 : PACKET]
    score = full[0:OWN] / (TEMPER * en * kn)
    count = recv_ref[:, 0, HALF:WIDE].T
    row = lax.broadcasted_iota(jnp.int32, (OWN, LANES), 0)
    lane = lax.broadcasted_iota(jnp.int32, (OWN, LANES), 1)
    spread = (row // ROWS == lane).astype(F32)
    count = dot(spread.astype(BF16), count.astype(BF16), NN)
    count = count + (lane == place[1]).astype(F32)
    ec = count * jnp.exp(score)
    z = jnp.sum(ec, axis=0, keepdims=True)
    s = jnp.sum(ec * score, axis=0, keepdims=True)
    blend = ec / kn
    coef_ref[...] = (SCALE / TEMPER) * blend / en
    kcoef_ref[...] = SCALE * ec * score / (kn * kn)
    send_ref[:, 0, 0:HALF] = dot(blend.T, bank_ref[...].astype(F32), NN, PRECISE)
    zs = jnp.where(row == 0, jnp.broadcast_to(z, (OWN, LANES)), jnp.broadcast_to(s, (OWN, LANES)))
    send_ref[:, 0, HALF:WIDE] = zs.T


def grad_body(place, recv_ref, emb_ref, pos_ref, scal_ref, slope_ref, mixed_ref, z_ref):
    total = jnp.sum(recv_ref[:, 0, :], axis=0, keepdims=True)
    esq = scal_ref[0:1, 0:1]
    inner = scal_ref[8:9, 0:1]
    psq = scal_ref[16:17, 0:1]
    en = jnp.sqrt(esq + EPSILON)
    pn = jnp.sqrt(psq + EPSILON)
    score = inner / (TEMPER * en * pn)
    hit = jnp.exp(score)
    z = total[:, HALF : HALF + 1] + hit
    s = total[:, HALF + 1 : HALF + 2] + hit * score
    row_weight = SCALE * (s / z - score)
    unit = emb_ref[0:1, :] / en
    pos = pos_ref[...].astype(F32)
    direction = (SCALE / TEMPER) * (total[:, 0:HALF] / z + ((hit / z - 1.0) / pn) * pos)
    grad = (direction - row_weight * unit) / en * (1.0 / LEN)
    for t in range(0, LEN, 32):
        mixed_ref[t : t + 32, :] = (slope_ref[t : t + 32, :] * grad).astype(BF16)
    lane = lax.broadcasted_iota(jnp.int32, (8, HALF), 1)
    z_ref[...] = jnp.where(lane == place[1], jnp.broadcast_to(z, (8, HALF)), 0.0)


def weight_body(
    place, mine_ref, theirs_ref, hidden_ref, w_ref, tokens_ref, z_ref, send_ref, pad, small
):
    fill_padded(tokens_ref, pad)
    g = place[0]
    first = pl.multiple_of(g * HALF, HALF)
    second = pl.multiple_of((1 - g) * HALF, HALF)
    hidden_grad = dot(mine_ref[...], w_ref[pl.ds(first, HALF), :], NN)
    hidden_grad = hidden_grad + dot(theirs_ref[...], w_ref[pl.ds(second, HALF), :], NN)
    for k in range(KW):
        small[k : k + 1, :] = jnp.sum(
            hidden_grad * pad[5 + k : 5 + k + LEN, :], axis=0, keepdims=True
        )
    small[KW : KW + 1, :] = z_ref[0:1, :]
    value = small[...]
    upper = value.astype(BF16).astype(F32)
    packed = jnp.concatenate([upper, value - upper], axis=0).astype(BF16)
    for p in range(PLANE):
        send_ref[p, Z_ROWS : Z_ROWS + PACK, :] = packed
    per = PLANE // 2
    mine = dot(mine_ref[...], hidden_ref[...], TN).astype(BF16)
    theirs = dot(theirs_ref[...], hidden_ref[...], TN).astype(BF16)
    for p in range(per):
        send_ref[g * per + p, 0:Z_ROWS, :] = mine[p * Z_ROWS : (p + 1) * Z_ROWS, :]
        send_ref[(1 - g) * per + p, 0:Z_ROWS, :] = theirs[p * Z_ROWS : (p + 1) * Z_ROWS, :]


BLOCK = OUT_ROWS + 8


def plane_body(recv_ref, send_ref, total):
    for r in range(0, Z_ROWS + PACK, 16):
        acc = recv_ref[0, r : r + 16, :].astype(F32)
        for p in range(1, PLANE):
            acc = acc + recv_ref[p, r : r + 16, :].astype(F32)
        total[r : r + 16, :] = acc
    rest = total[Z_ROWS : Z_ROWS + 8, :] + total[Z_ROWS + 8 : Z_ROWS + 16, :]
    for c in range(COLS):
        cols = slice(c * LANES, (c + 1) * LANES)
        for z in range(NZ):
            send_ref[z, c * BLOCK : c * BLOCK + OUT_ROWS, :] = total[
                z * OUT_ROWS : (z + 1) * OUT_ROWS, cols
            ]
            send_ref[z, c * BLOCK + OUT_ROWS : (c + 1) * BLOCK, :] = rest[:, cols]


def final_body(
    recv_ref, coef_ref, kcoef_ref, first_ref, bank_ref, bank_out, kernel_out, weight_out, total
):
    acc = recv_ref[0]
    for z in range(1, NZ):
        acc = acc + recv_ref[z]
    total[...] = acc
    for c in range(COLS):
        cols = slice(c * LANES, (c + 1) * LANES)
        base = c * BLOCK
        weight_out[:, cols] = total[base : base + OUT_ROWS, :] * (1.0 / N_DP)
        kernel_out[:, cols] = total[base + OUT_ROWS : base + OUT_ROWS + KW, :] * (1.0 / N_DP)
    inverse = 1.0 / total[BLOCK - 1 : BLOCK, :]
    coef = coef_ref[...] * inverse
    scale = jnp.sum(kcoef_ref[...] * inverse, axis=1, keepdims=True)
    product = dot(coef, first_ref[:, 0, 0:HALF], NN, PRECISE)
    bank_out[...] = product - scale * bank_ref[...].astype(F32)


def exchange(value, axes):
    return lax.all_to_all(value, axes, split_axis=0, concat_axis=0, tiled=True)


def per_device(tokens_in, dw_kernel, point_weight, positive_emb, bank, neg_owner, neg_block):
    tokens = tokens_in.reshape(LEN, HALF)
    g = lax.axis_index("group")
    d = (lax.axis_index("x") * NY + lax.axis_index("y")) * NZ + lax.axis_index("z")
    place = jnp.stack([g, d]).astype(jnp.int32)
    pad = pltpu.VMEM((LEN + 16, HALF), F32)
    flops = 2 * LEN * HALF * HALF

    hidden, other = call(
        conv_body,
        [((LEN, HALF), BF16), ((LEN, HALF), F32)],
        "conv_and_other_half",
        [pad],
        scalars=1,
        n_in=3,
        flops=flops,
    )(place, tokens, dw_kernel, point_weight)
    theirs = lax.ppermute(other, "group", SWAP)
    own, table = call(
        own_body,
        [((LEN, HALF), F32), ((N_DP, EXTRA), F32)],
        "own_half_and_requests",
        scalars=1,
        n_in=4,
        flops=flops,
    )(place, hidden, point_weight, neg_owner, neg_block.reshape(1, OWN))
    slope, emb, send = call(
        embed_body,
        [((LEN, HALF), F32), ((8, HALF), F32), ((N_DP, 1, WIDE), F32)],
        "embedding",
        n_in=4,
    )(own, theirs, tokens, table)
    gathered = exchange(send, DP)
    (packet,) = call(dots_body, [((PACKET, LANES), F32)], "inner_products", n_in=4)(
        gathered, bank, emb, positive_emb
    )
    packet_theirs = lax.ppermute(packet, "group", SWAP)
    send, coef, kcoef, scal = call(
        scores_body,
        [
            ((N_DP, 1, WIDE), F32),
            ((OWN, LANES), F32),
            ((OWN, LANES), F32),
            ((24, LANES), F32),
        ],
        "scores",
        scalars=1,
        n_in=4,
    )(place, packet, packet_theirs, gathered, bank)
    sums = exchange(send, DP)
    mixed, z = call(
        grad_body,
        [((LEN, HALF), BF16), ((8, HALF), F32)],
        "mixed_gradient",
        scalars=1,
        n_in=5,
    )(place, sums, emb, positive_emb, scal, slope)
    mixed_theirs = lax.ppermute(mixed, "group", SWAP)
    (send,) = call(
        weight_body,
        [((PLANE, Z_ROWS + PACK, HALF), BF16)],
        "weight_gradient",
        [pad, pltpu.VMEM((8, HALF), F32)],
        scalars=1,
        n_in=6,
    )(place, mixed, mixed_theirs, hidden, point_weight, tokens, z)
    planes = exchange(send, ("x", "y"))
    (send,) = call(
        plane_body,
        [((NZ, COLS * BLOCK, LANES), F32)],
        "sum_over_plane",
        [pltpu.VMEM((Z_ROWS + PACK, HALF), F32)],
        n_in=1,
    )(planes)
    lines = exchange(send, "z")
    return tuple(
        call(
            final_body,
            [((OWN, HALF), F32), ((KW, HALF), F32), ((OUT_ROWS, HALF), F32)],
            "outputs",
            [pltpu.VMEM((COLS * BLOCK, LANES), F32)],
            n_in=5,
        )(lines, coef, kcoef, gathered, bank)
    )


def solution(mesh):
    factored = Mesh(mesh.devices.reshape(NX, NY, NZ, 2), ("x", "y", "z", "group"))
    in_specs = (
        P(DP, None, "group"),
        P(None, "group"),
        P(None, "group"),
        P(DP, "group"),
        P(DP, "group"),
        P(DP, None),
        P(DP),
    )
    out_specs = (P(DP, "group"), P(None, "group"), P(DP, "group"))
    return jax.shard_map(
        per_device, mesh=factored, in_specs=in_specs, out_specs=out_specs, check_vma=False
    )
```

```python
import jax
import jax.numpy as jnp
from jax import lax
from jax.experimental import pallas as pl
from jax.experimental.pallas import tpu as pltpu
from jax.sharding import PartitionSpec as P

KW = 7
LEN = 256
HALF = 768
N_DP = 128
NX, NY, NZ = 4, 4, 8
PLANE = NX * NY
ROWS = 8
OWN = 128
OUT_ROWS = 12
Z_ROWS = OUT_ROWS * NZ
PACK = 8
SLOT = 8
LANES = 128
COLS = HALF // LANES

TEMPER = 0.07
SCALE = 256.0
EPSILON = 1e-06
GELU_C = 0.7978845608028654
GELU_A = 0.044715
PRECISE = lax.Precision.HIGHEST
F32 = jnp.float32
BF16 = jnp.bfloat16

DP = "dp"
PLANES = [[(x * NY + y) * NZ + z for x in range(NX) for y in range(NY)] for z in range(NZ)]
LINES = [[p * NZ + z for z in range(NZ)] for p in range(PLANE)]
SWAP = [(0, 1), (1, 0)]
VMEM_BYTES = 20 * 2**20

NT = (((1,), (1,)), ((), ()))
NN = (((1,), (0,)), ((), ()))
TN = (((0,), (0,)), ((), ()))


def dot(a, b, dims, precision=None):
    return lax.dot_general(a, b, dims, precision=precision, preferred_element_type=F32)


def call(body, outs, name, scratch=(), scalars=0, n_in=0, flops=0, in_hbm=0):
    smem = [pl.BlockSpec(memory_space=pltpu.SMEM)] * scalars
    vmem = [pl.BlockSpec(memory_space=pltpu.VMEM)] * n_in
    return pl.pallas_call(
        body,
        out_shape=[jax.ShapeDtypeStruct(s, d) for s, d in outs],
        in_specs=smem + [pl.BlockSpec(memory_space=pltpu.HBM)] * in_hbm + vmem,
        out_specs=[pl.BlockSpec(memory_space=pltpu.VMEM)] * len(outs),
        scratch_shapes=list(scratch),
        compiler_params=pltpu.CompilerParams(vmem_limit_bytes=VMEM_BYTES),
        cost_estimate=pl.CostEstimate(flops=flops, bytes_accessed=1 << 20, transcendentals=0),
        name=name,
    )


def fill_padded(tokens_ref, pad):
    pad[0:8, :] = jnp.zeros((8, HALF), F32)
    pad[LEN + 8 : LEN + 16, :] = jnp.zeros((8, HALF), F32)
    for t in range(0, LEN, 32):
        pad[8 + t : 40 + t, :] = tokens_ref[t : t + 32, :].astype(F32)


def conv_body(
    place, tokens_hbm, dw_hbm, w_hbm, hidden_ref, other_ref, pad, tokens_ref, dw_ref, w_ref, sems
):
    start = pl.multiple_of((1 - place[0]) * HALF, HALF)
    copies = [
        pltpu.make_async_copy(tokens_hbm, tokens_ref, sems.at[0]),
        pltpu.make_async_copy(dw_hbm, dw_ref, sems.at[1]),
        pltpu.make_async_copy(w_hbm.at[pl.ds(start, HALF), :], w_ref, sems.at[2]),
    ]
    for copy in copies:
        copy.start()
    copies[0].wait()
    fill_padded(tokens_ref, pad)
    copies[1].wait()
    for t in range(0, LEN, 32):
        total = jnp.zeros((32, HALF), F32)
        for k in range(KW):
            total = total + dw_ref[k : k + 1, :] * pad[5 + k + t : 37 + k + t, :]
        hidden_ref[t : t + 32, :] = total.astype(BF16)
    copies[2].wait()
    other_ref[...] = dot(hidden_ref[...], w_ref[...], NT)


def own_body(place, hidden_ref, w_ref, owner_ref, block_ref, own_ref, table_ref):
    start = pl.multiple_of(place[0] * HALF, HALF)
    own_ref[...] = dot(hidden_ref[...], w_ref[pl.ds(start, HALF), :], NT)
    lane = lax.broadcasted_iota(jnp.int32, (OWN, LANES), 1)
    named = (owner_ref[...] == lane).astype(F32)
    blocks = jnp.broadcast_to(block_ref[...].astype(F32), (LANES, OWN)).T
    wanted = (blocks == lane.astype(F32)).astype(F32)
    table_ref[...] = dot(named.T.astype(BF16), wanted.astype(BF16), NN)


def embed_body(own_ref, other_ref, tokens_ref, table_ref, slope_ref, emb_ref, send_ref, stage):
    total = jnp.zeros((8, HALF), F32)
    for t in range(0, LEN, 32):
        x = own_ref[t : t + 32, :] + other_ref[t : t + 32, :]
        sq = x * x
        th = jnp.tanh(GELU_C * x * (1.0 + GELU_A * sq))
        half = 0.5 * (1.0 + th)
        slope_ref[t : t + 32, :] = half + (0.5 * GELU_C) * x * (1.0 - th * th) * (
            1.0 + (3.0 * GELU_A) * sq
        )
        y = tokens_ref[t : t + 32, :].astype(F32) + x * half
        total = total + (y[0:8] + y[8:16]) + (y[16:24] + y[24:32])
    emb = jnp.sum(total, axis=0, keepdims=True) * (1.0 / LEN)
    emb_ref[...] = jnp.broadcast_to(emb, (8, HALF))
    for c in range(COLS):
        block = jnp.broadcast_to(emb[:, c * LANES : (c + 1) * LANES], (N_DP, LANES))
        stage[pl.ds(c, N_DP, stride=SLOT), :] = block
    stage[pl.ds(COLS, N_DP, stride=SLOT), :] = table_ref[...]
    stage[pl.ds(COLS + 1, N_DP, stride=SLOT), :] = jnp.zeros((N_DP, LANES), F32)
    send_ref[...] = stage[...].astype(BF16)


def dots_body(recv_ref, bank_ref, emb_ref, pos_ref, packet_ref, first_ref, count_ref, stage):
    stage[...] = recv_ref[...].astype(F32)
    for c in range(COLS):
        first_ref[:, c * LANES : (c + 1) * LANES] = stage[pl.ds(c, N_DP, stride=SLOT), :]
    count_ref[...] = stage[pl.ds(COLS, N_DP, stride=SLOT), :]
    e = first_ref[...]
    key = bank_ref[...].astype(F32)
    packet_ref[0:OWN, :] = dot(bank_ref[...], e.astype(BF16), NT)
    ones = jnp.ones((8, HALF), F32)
    packet_ref[OWN : OWN + 8, :] = dot(ones, e * e, NT, PRECISE)
    ksq = jnp.sum(key * key, axis=1, keepdims=True)
    packet_ref[OWN + 8 : 2 * OWN + 8, :] = jnp.broadcast_to(ksq, (OWN, LANES))
    emb = emb_ref[0:1, :]
    pos = pos_ref[...].astype(F32)
    rows = (emb * emb, emb * pos, pos * pos)
    for i in range(3):
        value = jnp.sum(rows[i], axis=1, keepdims=True)
        packet_ref[2 * OWN + 8 + 8 * i : 2 * OWN + 16 + 8 * i, :] = jnp.broadcast_to(
            value, (8, LANES)
        )


PACKET = 2 * OWN + 32


def scores_body(
    place, mine_ref, theirs_ref, count_ref, bank_ref, send_ref, coef_ref, kcoef_ref, scal_ref, stage
):
    full = mine_ref[...] + theirs_ref[...]
    en = jnp.sqrt(full[OWN : OWN + 1] + EPSILON)
    kn = jnp.sqrt(full[OWN + 8 : 2 * OWN + 8] + EPSILON)
    scal_ref[...] = full[2 * OWN + 8 : PACKET]
    score = full[0:OWN] / (TEMPER * en * kn)
    count = count_ref[...].T
    row = lax.broadcasted_iota(jnp.int32, (OWN, LANES), 0)
    lane = lax.broadcasted_iota(jnp.int32, (OWN, LANES), 1)
    spread = (row // ROWS == lane).astype(F32)
    count = dot(spread.astype(BF16), count.astype(BF16), NN)
    count = count + (lane == place[1]).astype(F32)
    ec = count * jnp.exp(score)
    z = jnp.sum(ec, axis=0, keepdims=True)
    s = jnp.sum(ec * score, axis=0, keepdims=True)
    blend = ec / kn
    coef_ref[...] = (SCALE / TEMPER) * blend / en
    kcoef_ref[...] = SCALE * ec * score / (kn * kn)
    sums = dot(blend.T, bank_ref[...].astype(F32), NN, PRECISE)
    for c in range(COLS):
        stage[pl.ds(c, N_DP, stride=SLOT), :] = sums[:, c * LANES : (c + 1) * LANES]
    zs = jnp.zeros((OWN, LANES), F32)
    for i, value in enumerate((z, s)):
        upper = value.astype(BF16).astype(F32)
        zs = jnp.where(row == 2 * i, jnp.broadcast_to(upper, (OWN, LANES)), zs)
        zs = jnp.where(row == 2 * i + 1, jnp.broadcast_to(value - upper, (OWN, LANES)), zs)
    stage[pl.ds(COLS, N_DP, stride=SLOT), :] = zs.T
    stage[pl.ds(COLS + 1, N_DP, stride=SLOT), :] = jnp.zeros((N_DP, LANES), F32)
    send_ref[...] = stage[...].astype(BF16)


def grad_body(place, recv_ref, emb_ref, pos_ref, scal_ref, slope_ref, mixed_ref, z_ref):
    acc = jnp.zeros((2 * SLOT, LANES), F32)
    for i in range(0, N_DP * SLOT, 2 * SLOT):
        acc = acc + recv_ref[i : i + 2 * SLOT, :].astype(F32)
    acc = acc[0:SLOT] + acc[SLOT : 2 * SLOT]
    total = jnp.concatenate([acc[c : c + 1] for c in range(COLS)], axis=1)
    tail = acc[COLS : COLS + 1]
    esq = scal_ref[0:1, 0:1]
    inner = scal_ref[8:9, 0:1]
    psq = scal_ref[16:17, 0:1]
    en = jnp.sqrt(esq + EPSILON)
    pn = jnp.sqrt(psq + EPSILON)
    score = inner / (TEMPER * en * pn)
    hit = jnp.exp(score)
    z = tail[:, 0:1] + tail[:, 1:2] + hit
    s = tail[:, 2:3] + tail[:, 3:4] + hit * score
    row_weight = SCALE * (s / z - score)
    unit = emb_ref[0:1, :] / en
    pos = pos_ref[...].astype(F32)
    direction = (SCALE / TEMPER) * (total / z + ((hit / z - 1.0) / pn) * pos)
    grad = (direction - row_weight * unit) / en * (1.0 / LEN)
    for t in range(0, LEN, 32):
        mixed_ref[t : t + 32, :] = (slope_ref[t : t + 32, :] * grad).astype(BF16)
    upper = z.astype(BF16).astype(F32)
    lane = lax.broadcasted_iota(jnp.int32, (8, HALF), 1)
    line = jnp.where(lane == place[1], jnp.broadcast_to(upper, (8, HALF)), 0.0)
    z_ref[...] = jnp.where(lane == place[1] + LANES, jnp.broadcast_to(z - upper, (8, HALF)), line)


def weight_body(
    place, mine_ref, theirs_ref, hidden_ref, w_ref, tokens_ref, z_ref, send_ref, pad, small
):
    fill_padded(tokens_ref, pad)
    g = place[0]
    first = pl.multiple_of(g * HALF, HALF)
    second = pl.multiple_of((1 - g) * HALF, HALF)
    hidden_grad = dot(mine_ref[...], w_ref[pl.ds(first, HALF), :], NN)
    hidden_grad = hidden_grad + dot(theirs_ref[...], w_ref[pl.ds(second, HALF), :], NN)
    for k in range(KW):
        small[k : k + 1, :] = jnp.sum(
            hidden_grad * pad[5 + k : 5 + k + LEN, :], axis=0, keepdims=True
        )
    small[KW : KW + 1, :] = z_ref[0:1, :]
    extra = small[...]
    per = PLANE // 2
    for side, ref in ((g, mine_ref), (1 - g, theirs_ref)):
        product = dot(ref[...], hidden_ref[...], TN)
        for p in range(per):
            rows = product[p * Z_ROWS : (p + 1) * Z_ROWS, :]
            send_ref[side * per + p] = jnp.concatenate([rows, extra], axis=0).astype(BF16)


BLOCK = OUT_ROWS + 8


def plane_body(recv_ref, send_ref, total):
    for c in range(COLS):
        cols = slice(c * LANES, (c + 1) * LANES)
        acc = recv_ref[0, :, cols].astype(F32)
        for p in range(1, PLANE):
            acc = acc + recv_ref[p, :, cols].astype(F32)
        total[:, cols] = acc
    last = Z_ROWS + PACK - 1
    total[last : last + 1, 0:LANES] = (
        total[last : last + 1, 0:LANES] + total[last : last + 1, LANES : 2 * LANES]
    )
    for c in range(COLS):
        cols = slice(c * LANES, (c + 1) * LANES)
        for z in range(NZ):
            send_ref[z, c * BLOCK : c * BLOCK + OUT_ROWS, :] = total[
                z * OUT_ROWS : (z + 1) * OUT_ROWS, cols
            ]
            send_ref[z, c * BLOCK + OUT_ROWS : (c + 1) * BLOCK, :] = total[
                Z_ROWS : Z_ROWS + PACK, cols
            ]


def final_body(
    recv_ref, coef_ref, kcoef_ref, first_ref, bank_ref, bank_out, kernel_out, weight_out, total
):
    acc = recv_ref[0]
    for z in range(1, NZ):
        acc = acc + recv_ref[z]
    total[...] = acc
    for c in range(COLS):
        cols = slice(c * LANES, (c + 1) * LANES)
        base = c * BLOCK
        weight_out[:, cols] = total[base : base + OUT_ROWS, :] * (1.0 / N_DP)
        kernel_out[:, cols] = total[base + OUT_ROWS : base + OUT_ROWS + KW, :] * (1.0 / N_DP)
    inverse = 1.0 / total[BLOCK - 1 : BLOCK, :]
    coef = coef_ref[...] * inverse
    scale = jnp.sum(kcoef_ref[...] * inverse, axis=1, keepdims=True)
    product = dot(coef, first_ref[...], NN, PRECISE)
    bank_out[...] = product - scale * bank_ref[...].astype(F32)


def exchange(value, groups=None):
    return lax.all_to_all(
        value, DP, split_axis=0, concat_axis=0, tiled=True, axis_index_groups=groups
    )


def exchange_slots(value):
    return exchange(value.reshape(N_DP, SLOT, LANES)).reshape(N_DP * SLOT, LANES)


def per_device(tokens_in, dw_kernel, point_weight, positive_emb, bank, neg_owner, neg_block):
    tokens = tokens_in.reshape(LEN, HALF)
    g = lax.axis_index("group")
    d = lax.axis_index(DP)
    place = jnp.stack([g, d]).astype(jnp.int32)
    pad = pltpu.VMEM((LEN + 16, HALF), F32)
    stage = pltpu.VMEM((N_DP * SLOT, LANES), F32)
    flops = 2 * LEN * HALF * HALF

    hidden, other = call(
        conv_body,
        [((LEN, HALF), BF16), ((LEN, HALF), F32)],
        "conv_and_other_half",
        [
            pad,
            pltpu.VMEM((LEN, HALF), BF16),
            pltpu.VMEM((KW, HALF), F32),
            pltpu.VMEM((HALF, HALF), BF16),
            pltpu.SemaphoreType.DMA((3,)),
        ],
        scalars=1,
        in_hbm=3,
        flops=flops,
    )(place, tokens, dw_kernel, point_weight)
    theirs = lax.ppermute(other, "group", SWAP)
    own, table = call(
        own_body,
        [((LEN, HALF), F32), ((N_DP, LANES), F32)],
        "own_half_and_requests",
        scalars=1,
        n_in=4,
        flops=flops,
    )(place, hidden, point_weight, neg_owner, neg_block.reshape(1, OWN))
    slope, emb, send = call(
        embed_body,
        [((LEN, HALF), F32), ((8, HALF), F32), ((N_DP * SLOT, LANES), BF16)],
        "embedding",
        [stage],
        n_in=4,
    )(own, theirs, tokens, table)
    gathered = exchange_slots(send)
    packet, first, count = call(
        dots_body,
        [((PACKET, LANES), F32), ((N_DP, HALF), F32), ((N_DP, LANES), F32)],
        "inner_products",
        [stage],
        n_in=4,
    )(gathered, bank, emb, positive_emb)
    packet_theirs = lax.ppermute(packet, "group", SWAP)
    send, coef, kcoef, scal = call(
        scores_body,
        [
            ((N_DP * SLOT, LANES), BF16),
            ((OWN, LANES), F32),
            ((OWN, LANES), F32),
            ((24, LANES), F32),
        ],
        "scores",
        [stage],
        scalars=1,
        n_in=4,
    )(place, packet, packet_theirs, count, bank)
    sums = exchange_slots(send)
    mixed, z = call(
        grad_body,
        [((LEN, HALF), BF16), ((8, HALF), F32)],
        "mixed_gradient",
        scalars=1,
        n_in=5,
    )(place, sums, emb, positive_emb, scal, slope)
    mixed_theirs = lax.ppermute(mixed, "group", SWAP)
    (send,) = call(
        weight_body,
        [((PLANE, Z_ROWS + PACK, HALF), BF16)],
        "weight_gradient",
        [pad, pltpu.VMEM((8, HALF), F32)],
        scalars=1,
        n_in=6,
    )(place, mixed, mixed_theirs, hidden, point_weight, tokens, z)
    planes = exchange(send, PLANES)
    (send,) = call(
        plane_body,
        [((NZ, COLS * BLOCK, LANES), F32)],
        "sum_over_plane",
        [pltpu.VMEM((Z_ROWS + PACK, HALF), F32)],
        n_in=1,
    )(planes)
    lines = exchange(send, LINES)
    return tuple(
        call(
            final_body,
            [((OWN, HALF), F32), ((KW, HALF), F32), ((OUT_ROWS, HALF), F32)],
            "outputs",
            [pltpu.VMEM((COLS * BLOCK, LANES), F32)],
            n_in=5,
        )(lines, coef, kcoef, first, bank)
    )


def solution(mesh):
    in_specs = (
        P(DP, None, "group"),
        P(None, "group"),
        P(None, "group"),
        P(DP, "group"),
        P(DP, "group"),
        P(DP, None),
        P(DP),
    )
    out_specs = (P(DP, "group"), P(None, "group"), P(DP, "group"))
    return jax.shard_map(
        per_device, mesh=mesh, in_specs=in_specs, out_specs=out_specs, check_vma=False
    )
```

```python
import jax
import jax.numpy as jnp
from jax import lax
from jax.experimental import pallas as pl
from jax.experimental.pallas import tpu as pltpu
from jax.sharding import PartitionSpec as P

KW = 7
LEN = 256
HALF = 768
N_DP = 128
NX, NY, NZ = 4, 4, 8
PLANE = NX * NY
ROWS = 8
OWN = 128
OUT_ROWS = 12
Z_ROWS = OUT_ROWS * NZ
PACK = 8
SLOT = 8
LANES = 128
COLS = HALF // LANES

TEMPER = 0.07
SCALE = 256.0
EPSILON = 1e-06
GELU_C = 0.7978845608028654
GELU_A = 0.044715
PRECISE = lax.Precision.HIGHEST
F32 = jnp.float32
BF16 = jnp.bfloat16

DP = "dp"
PLANES = [[(x * NY + y) * NZ + z for x in range(NX) for y in range(NY)] for z in range(NZ)]
LINES = [[p * NZ + z for z in range(NZ)] for p in range(PLANE)]
SWAP = [(0, 1), (1, 0)]
VMEM_BYTES = 20 * 2**20

NT = (((1,), (1,)), ((), ()))
NN = (((1,), (0,)), ((), ()))
TN = (((0,), (0,)), ((), ()))


def dot(a, b, dims, precision=None):
    return lax.dot_general(a, b, dims, precision=precision, preferred_element_type=F32)


def call(body, outs, name, scratch=(), scalars=0, n_in=0, flops=0, moved=1 << 20):
    smem = [pl.BlockSpec(memory_space=pltpu.SMEM)] * scalars
    vmem = [pl.BlockSpec(memory_space=pltpu.VMEM)] * n_in
    return pl.pallas_call(
        body,
        out_shape=[jax.ShapeDtypeStruct(s, d) for s, d in outs],
        in_specs=smem + vmem,
        out_specs=[pl.BlockSpec(memory_space=pltpu.VMEM)] * len(outs),
        scratch_shapes=list(scratch),
        compiler_params=pltpu.CompilerParams(vmem_limit_bytes=VMEM_BYTES),
        cost_estimate=pl.CostEstimate(flops=flops, bytes_accessed=moved, transcendentals=0),
        name=name,
    )


def fill_padded(tokens_ref, pad):
    pad[0:8, :] = jnp.zeros((8, HALF), F32)
    pad[LEN + 8 : LEN + 16, :] = jnp.zeros((8, HALF), F32)
    for t in range(0, LEN, 32):
        pad[8 + t : 40 + t, :] = tokens_ref[t : t + 32, :].astype(F32)


def conv_body(tokens_ref, dw_ref, hidden_ref, pad):
    fill_padded(tokens_ref, pad)
    for t in range(0, LEN, 32):
        total = jnp.zeros((32, HALF), F32)
        for k in range(KW):
            total = total + dw_ref[k : k + 1, :] * pad[5 + k + t : 37 + k + t, :]
        hidden_ref[t : t + 32, :] = total.astype(BF16)


def other_body(place, hidden_ref, w_ref, other_ref):
    start = pl.multiple_of((1 - place[0]) * HALF, HALF)
    other_ref[...] = dot(hidden_ref[...], w_ref[pl.ds(start, HALF), :], NT)


def own_body(place, hidden_ref, w_ref, owner_ref, block_ref, own_ref, table_ref):
    start = pl.multiple_of(place[0] * HALF, HALF)
    own_ref[...] = dot(hidden_ref[...], w_ref[pl.ds(start, HALF), :], NT)
    lane = lax.broadcasted_iota(jnp.int32, (OWN, LANES), 1)
    named = (owner_ref[...] == lane).astype(F32)
    blocks = jnp.broadcast_to(block_ref[...].astype(F32), (LANES, OWN)).T
    wanted = (blocks == lane.astype(F32)).astype(F32)
    table_ref[...] = dot(named.T.astype(BF16), wanted.astype(BF16), NN)


def embed_body(own_ref, other_ref, tokens_ref, table_ref, slope_ref, emb_ref, send_ref, stage):
    total = jnp.zeros((8, HALF), F32)
    for t in range(0, LEN, 32):
        x = own_ref[t : t + 32, :] + other_ref[t : t + 32, :]
        sq = x * x
        th = jnp.tanh(GELU_C * x * (1.0 + GELU_A * sq))
        half = 0.5 * (1.0 + th)
        slope_ref[t : t + 32, :] = half + (0.5 * GELU_C) * x * (1.0 - th * th) * (
            1.0 + (3.0 * GELU_A) * sq
        )
        y = tokens_ref[t : t + 32, :].astype(F32) + x * half
        total = total + (y[0:8] + y[8:16]) + (y[16:24] + y[24:32])
    emb = jnp.sum(total, axis=0, keepdims=True) * (1.0 / LEN)
    emb_ref[...] = jnp.broadcast_to(emb, (8, HALF))
    for c in range(COLS):
        block = jnp.broadcast_to(emb[:, c * LANES : (c + 1) * LANES], (N_DP, LANES))
        stage[pl.ds(c, N_DP, stride=SLOT), :] = block
    stage[pl.ds(COLS, N_DP, stride=SLOT), :] = table_ref[...]
    stage[pl.ds(COLS + 1, N_DP, stride=SLOT), :] = jnp.zeros((N_DP, LANES), F32)
    send_ref[...] = stage[...].astype(BF16)


def dots_body(recv_ref, bank_ref, emb_ref, pos_ref, packet_ref, first_ref, count_ref, stage):
    stage[...] = recv_ref[...].astype(F32)
    for c in range(COLS):
        first_ref[:, c * LANES : (c + 1) * LANES] = stage[pl.ds(c, N_DP, stride=SLOT), :]
    count_ref[...] = stage[pl.ds(COLS, N_DP, stride=SLOT), :]
    e = first_ref[...]
    key = bank_ref[...].astype(F32)
    packet_ref[0:OWN, :] = dot(bank_ref[...], e.astype(BF16), NT)
    ones = jnp.ones((8, HALF), F32)
    packet_ref[OWN : OWN + 8, :] = dot(ones, e * e, NT, PRECISE)
    ksq = jnp.sum(key * key, axis=1, keepdims=True)
    packet_ref[OWN + 8 : 2 * OWN + 8, :] = jnp.broadcast_to(ksq, (OWN, LANES))
    emb = emb_ref[0:1, :]
    pos = pos_ref[...].astype(F32)
    rows = (emb * emb, emb * pos, pos * pos)
    for i in range(3):
        value = jnp.sum(rows[i], axis=1, keepdims=True)
        packet_ref[2 * OWN + 8 + 8 * i : 2 * OWN + 16 + 8 * i, :] = jnp.broadcast_to(
            value, (8, LANES)
        )


PACKET = 2 * OWN + 32


def scores_body(
    place, mine_ref, theirs_ref, count_ref, bank_ref, send_ref, coef_ref, kcoef_ref, scal_ref, stage
):
    full = mine_ref[...] + theirs_ref[...]
    en = jnp.sqrt(full[OWN : OWN + 1] + EPSILON)
    kn = jnp.sqrt(full[OWN + 8 : 2 * OWN + 8] + EPSILON)
    scal_ref[...] = full[2 * OWN + 8 : PACKET]
    score = full[0:OWN] / (TEMPER * en * kn)
    count = count_ref[...].T
    row = lax.broadcasted_iota(jnp.int32, (OWN, LANES), 0)
    lane = lax.broadcasted_iota(jnp.int32, (OWN, LANES), 1)
    spread = (row // ROWS == lane).astype(F32)
    count = dot(spread.astype(BF16), count.astype(BF16), NN)
    count = count + (lane == place[1]).astype(F32)
    ec = count * jnp.exp(score)
    z = jnp.sum(ec, axis=0, keepdims=True)
    s = jnp.sum(ec * score, axis=0, keepdims=True)
    blend = ec / kn
    coef_ref[...] = (SCALE / TEMPER) * blend / en
    kcoef_ref[...] = SCALE * ec * score / (kn * kn)
    sums = dot(blend.T, bank_ref[...].astype(F32), NN, PRECISE)
    for c in range(COLS):
        stage[pl.ds(c, N_DP, stride=SLOT), :] = sums[:, c * LANES : (c + 1) * LANES]
    zs = jnp.zeros((OWN, LANES), F32)
    for i, value in enumerate((z, s)):
        upper = value.astype(BF16).astype(F32)
        zs = jnp.where(row == 2 * i, jnp.broadcast_to(upper, (OWN, LANES)), zs)
        zs = jnp.where(row == 2 * i + 1, jnp.broadcast_to(value - upper, (OWN, LANES)), zs)
    stage[pl.ds(COLS, N_DP, stride=SLOT), :] = zs.T
    stage[pl.ds(COLS + 1, N_DP, stride=SLOT), :] = jnp.zeros((N_DP, LANES), F32)
    send_ref[...] = stage[...].astype(BF16)


def grad_body(place, recv_ref, emb_ref, pos_ref, scal_ref, slope_ref, mixed_ref, z_ref):
    acc = jnp.zeros((2 * SLOT, LANES), F32)
    for i in range(0, N_DP * SLOT, 2 * SLOT):
        acc = acc + recv_ref[i : i + 2 * SLOT, :].astype(F32)
    acc = acc[0:SLOT] + acc[SLOT : 2 * SLOT]
    total = jnp.concatenate([acc[c : c + 1] for c in range(COLS)], axis=1)
    tail = acc[COLS : COLS + 1]
    esq = scal_ref[0:1, 0:1]
    inner = scal_ref[8:9, 0:1]
    psq = scal_ref[16:17, 0:1]
    en = jnp.sqrt(esq + EPSILON)
    pn = jnp.sqrt(psq + EPSILON)
    score = inner / (TEMPER * en * pn)
    hit = jnp.exp(score)
    z = tail[:, 0:1] + tail[:, 1:2] + hit
    s = tail[:, 2:3] + tail[:, 3:4] + hit * score
    row_weight = SCALE * (s / z - score)
    unit = emb_ref[0:1, :] / en
    pos = pos_ref[...].astype(F32)
    direction = (SCALE / TEMPER) * (total / z + ((hit / z - 1.0) / pn) * pos)
    grad = (direction - row_weight * unit) / en * (1.0 / LEN)
    for t in range(0, LEN, 32):
        mixed_ref[t : t + 32, :] = (slope_ref[t : t + 32, :] * grad).astype(BF16)
    upper = z.astype(BF16).astype(F32)
    lane = lax.broadcasted_iota(jnp.int32, (8, HALF), 1)
    line = jnp.where(lane == place[1], jnp.broadcast_to(upper, (8, HALF)), 0.0)
    z_ref[...] = jnp.where(lane == place[1] + LANES, jnp.broadcast_to(z - upper, (8, HALF)), line)


def mine_body(place, mine_ref, hidden_ref, w_ref, product_ref, part_ref):
    g = place[0]
    first = pl.multiple_of(g * HALF, HALF)
    part_ref[...] = dot(mine_ref[...], w_ref[pl.ds(first, HALF), :], NN)
    product_ref[...] = dot(mine_ref[...], hidden_ref[...], TN)


def weight_body(
    place, theirs_ref, hidden_ref, w_ref, tokens_ref, z_ref, part_ref, mine_ref, send_ref, pad, small
):
    fill_padded(tokens_ref, pad)
    g = place[0]
    second = pl.multiple_of((1 - g) * HALF, HALF)
    hidden_grad = part_ref[...] + dot(theirs_ref[...], w_ref[pl.ds(second, HALF), :], NN)
    for k in range(KW):
        small[k : k + 1, :] = jnp.sum(
            hidden_grad * pad[5 + k : 5 + k + LEN, :], axis=0, keepdims=True
        )
    small[KW : KW + 1, :] = z_ref[0:1, :]
    extra = small[...]
    product = dot(theirs_ref[...], hidden_ref[...], TN)
    per = PLANE // 2
    for p in range(per):
        span = slice(p * Z_ROWS, (p + 1) * Z_ROWS)
        for side, rows in ((g, mine_ref[span, :]), (1 - g, product[span, :])):
            send_ref[side * per + p] = jnp.concatenate([rows, extra], axis=0).astype(BF16)


BLOCK = OUT_ROWS + 8


def plane_body(recv_ref, send_ref, total, stage):
    for c in range(COLS):
        cols = slice(c * LANES, (c + 1) * LANES)
        acc = recv_ref[0, :, cols].astype(F32)
        for p in range(1, PLANE):
            acc = acc + recv_ref[p, :, cols].astype(F32)
        total[:, cols] = acc
    for c in range(COLS):
        cols = slice(c * LANES, (c + 1) * LANES)
        for z in range(NZ):
            stage[z, c * BLOCK : c * BLOCK + OUT_ROWS, :] = total[
                z * OUT_ROWS : (z + 1) * OUT_ROWS, cols
            ]
            stage[z, c * BLOCK + OUT_ROWS : (c + 1) * BLOCK, :] = total[
                Z_ROWS : Z_ROWS + PACK, cols
            ]
    send_ref[...] = stage[...].astype(BF16)


def final_body(
    recv_ref, coef_ref, kcoef_ref, first_ref, bank_ref, bank_out, kernel_out, weight_out, total
):
    acc = recv_ref[0].astype(F32)
    for z in range(1, NZ):
        acc = acc + recv_ref[z].astype(F32)
    total[...] = acc
    for c in range(COLS):
        cols = slice(c * LANES, (c + 1) * LANES)
        base = c * BLOCK
        weight_out[:, cols] = total[base : base + OUT_ROWS, :] * (1.0 / N_DP)
        kernel_out[:, cols] = total[base + OUT_ROWS : base + OUT_ROWS + KW, :] * (1.0 / N_DP)
    inverse = 1.0 / (total[BLOCK - 1 : BLOCK, :] + total[2 * BLOCK - 1 : 2 * BLOCK, :])
    coef = coef_ref[...] * inverse
    scale = jnp.sum(kcoef_ref[...] * inverse, axis=1, keepdims=True)
    product = dot(coef, first_ref[...], NN, PRECISE)
    bank_out[...] = product - scale * bank_ref[...].astype(F32)


def exchange(value, groups=None):
    return lax.all_to_all(
        value, DP, split_axis=0, concat_axis=0, tiled=True, axis_index_groups=groups
    )


def exchange_slots(value):
    return exchange(value.reshape(N_DP, SLOT, LANES)).reshape(N_DP * SLOT, LANES)


def per_device(tokens_in, dw_kernel, point_weight, positive_emb, bank, neg_owner, neg_block):
    tokens = tokens_in.reshape(LEN, HALF)
    g = lax.axis_index("group")
    d = lax.axis_index(DP)
    place = jnp.stack([g, d]).astype(jnp.int32)
    pad = pltpu.VMEM((LEN + 16, HALF), F32)
    stage = pltpu.VMEM((N_DP * SLOT, LANES), F32)
    flops = 2 * LEN * HALF * HALF

    (hidden,) = call(conv_body, [((LEN, HALF), BF16)], "convolution", [pad], n_in=2, moved=16 << 20)(
        tokens, dw_kernel
    )
    (other,) = call(
        other_body, [((LEN, HALF), F32)], "other_half", scalars=1, n_in=2, flops=flops
    )(place, hidden, point_weight)
    theirs = lax.ppermute(other, "group", SWAP)
    own, table = call(
        own_body,
        [((LEN, HALF), F32), ((N_DP, LANES), F32)],
        "own_half_and_requests",
        scalars=1,
        n_in=4,
        flops=flops,
    )(place, hidden, point_weight, neg_owner, neg_block.reshape(1, OWN))
    slope, emb, send = call(
        embed_body,
        [((LEN, HALF), F32), ((8, HALF), F32), ((N_DP * SLOT, LANES), BF16)],
        "embedding",
        [stage],
        n_in=4,
    )(own, theirs, tokens, table)
    gathered = exchange_slots(send)
    packet, first, count = call(
        dots_body,
        [((PACKET, LANES), F32), ((N_DP, HALF), F32), ((N_DP, LANES), F32)],
        "inner_products",
        [stage],
        n_in=4,
    )(gathered, bank, emb, positive_emb)
    packet_theirs = lax.ppermute(packet, "group", SWAP)
    send, coef, kcoef, scal = call(
        scores_body,
        [
            ((N_DP * SLOT, LANES), BF16),
            ((OWN, LANES), F32),
            ((OWN, LANES), F32),
            ((24, LANES), F32),
        ],
        "scores",
        [stage],
        scalars=1,
        n_in=4,
    )(place, packet, packet_theirs, count, bank)
    sums = exchange_slots(send)
    mixed, z = call(
        grad_body,
        [((LEN, HALF), BF16), ((8, HALF), F32)],
        "mixed_gradient",
        scalars=1,
        n_in=5,
    )(place, sums, emb, positive_emb, scal, slope)
    mixed_theirs = lax.ppermute(mixed, "group", SWAP)
    product, part = call(
        mine_body,
        [((HALF, HALF), F32), ((LEN, HALF), F32)],
        "weight_gradient_own_half",
        scalars=1,
        n_in=3,
        flops=2 * flops,
    )(place, mixed, hidden, point_weight)
    (send,) = call(
        weight_body,
        [((PLANE, Z_ROWS + PACK, HALF), BF16)],
        "weight_gradient",
        [pad, pltpu.VMEM((8, HALF), F32)],
        scalars=1,
        n_in=7,
        flops=2 * flops,
    )(place, mixed_theirs, hidden, point_weight, tokens, z, part, product)
    planes = exchange(send, PLANES)
    (send,) = call(
        plane_body,
        [((NZ, COLS * BLOCK, LANES), BF16)],
        "sum_over_plane",
        [pltpu.VMEM((Z_ROWS + PACK, HALF), F32), pltpu.VMEM((NZ, COLS * BLOCK, LANES), F32)],
        n_in=1,
    )(planes)
    lines = exchange(send, LINES)
    return tuple(
        call(
            final_body,
            [((OWN, HALF), F32), ((KW, HALF), F32), ((OUT_ROWS, HALF), F32)],
            "outputs",
            [pltpu.VMEM((COLS * BLOCK, LANES), F32)],
            n_in=5,
        )(lines, coef, kcoef, first, bank)
    )


def solution(mesh):
    in_specs = (
        P(DP, None, "group"),
        P(None, "group"),
        P(None, "group"),
        P(DP, "group"),
        P(DP, "group"),
        P(DP, None),
        P(DP),
    )
    out_specs = (P(DP, "group"), P(None, "group"), P(DP, "group"))
    return jax.shard_map(
        per_device, mesh=mesh, in_specs=in_specs, out_specs=out_specs, check_vma=False
    )
```

```python
import jax
import jax.numpy as jnp
from jax import lax
from jax.experimental import pallas as pl
from jax.experimental.pallas import tpu as pltpu
from jax.sharding import PartitionSpec as P

KW = 7
LEN = 256
HALF = 768
N_DP = 128
NX, NY, NZ = 4, 4, 8
PLANE = NX * NY
ROWS = 8
OWN = 128
OUT_ROWS = 12
Z_ROWS = OUT_ROWS * NZ
PACK = 8
SLOT = 8
LANES = 128
COLS = HALF // LANES

TEMPER = 0.07
SCALE = 256.0
EPSILON = 1e-06
GELU_C = 0.7978845608028654
GELU_A = 0.044715
PRECISE = lax.Precision.HIGHEST
F32 = jnp.float32
BF16 = jnp.bfloat16

DP = "dp"
PLANES = [[(x * NY + y) * NZ + z for x in range(NX) for y in range(NY)] for z in range(NZ)]
LINES = [[p * NZ + z for z in range(NZ)] for p in range(PLANE)]
SWAP = [(0, 1), (1, 0)]
VMEM_BYTES = 20 * 2**20

NT = (((1,), (1,)), ((), ()))
NN = (((1,), (0,)), ((), ()))
TN = (((0,), (0,)), ((), ()))


def dot(a, b, dims, precision=None):
    return lax.dot_general(a, b, dims, precision=precision, preferred_element_type=F32)


def call(body, outs, name, scratch=(), scalars=0, n_in=0, flops=0, moved=1 << 20, in_hbm=0, limit=VMEM_BYTES):
    smem = [pl.BlockSpec(memory_space=pltpu.SMEM)] * scalars
    vmem = [pl.BlockSpec(memory_space=pltpu.VMEM)] * n_in
    return pl.pallas_call(
        body,
        out_shape=[jax.ShapeDtypeStruct(s, d) for s, d in outs],
        in_specs=smem + [pl.BlockSpec(memory_space=pl.ANY)] * in_hbm + vmem,
        out_specs=[pl.BlockSpec(memory_space=pltpu.VMEM)] * len(outs),
        scratch_shapes=list(scratch),
        compiler_params=pltpu.CompilerParams(vmem_limit_bytes=limit),
        cost_estimate=pl.CostEstimate(flops=flops, bytes_accessed=moved, transcendentals=0),
        name=name,
    )


def fill_padded(tokens_ref, pad):
    pad[0:8, :] = jnp.zeros((8, HALF), F32)
    pad[LEN + 8 : LEN + 16, :] = jnp.zeros((8, HALF), F32)
    for t in range(0, LEN, 32):
        pad[8 + t : 40 + t, :] = tokens_ref[t : t + 32, :].astype(F32)


def conv_body(place, w_hbm, tokens_ref, dw_ref, hidden_ref, other_ref, pad, w_ref, sem):
    start = pl.multiple_of((1 - place[0]) * HALF, HALF)
    copy = pltpu.make_async_copy(w_hbm.at[pl.ds(start, HALF), :], w_ref, sem)
    copy.start()
    fill_padded(tokens_ref, pad)
    for t in range(0, LEN, 32):
        total = jnp.zeros((32, HALF), F32)
        for k in range(KW):
            total = total + dw_ref[k : k + 1, :] * pad[5 + k + t : 37 + k + t, :]
        hidden_ref[t : t + 32, :] = total.astype(BF16)
    copy.wait()
    other_ref[...] = dot(hidden_ref[...], w_ref[...], NT)


def own_body(place, hidden_ref, w_ref, owner_ref, block_ref, own_ref, table_ref):
    start = pl.multiple_of(place[0] * HALF, HALF)
    own_ref[...] = dot(hidden_ref[...], w_ref[pl.ds(start, HALF), :], NT)
    lane = lax.broadcasted_iota(jnp.int32, (OWN, LANES), 1)
    named = (owner_ref[...] == lane).astype(F32)
    blocks = jnp.broadcast_to(block_ref[...].astype(F32), (LANES, OWN)).T
    wanted = (blocks == lane.astype(F32)).astype(F32)
    table_ref[...] = dot(named.T.astype(BF16), wanted.astype(BF16), NN)


def embed_body(own_ref, other_ref, tokens_ref, table_ref, slope_ref, emb_ref, send_ref, stage):
    total = jnp.zeros((8, HALF), F32)
    for t in range(0, LEN, 32):
        x = own_ref[t : t + 32, :] + other_ref[t : t + 32, :]
        sq = x * x
        th = jnp.tanh(GELU_C * x * (1.0 + GELU_A * sq))
        half = 0.5 * (1.0 + th)
        slope_ref[t : t + 32, :] = half + (0.5 * GELU_C) * x * (1.0 - th * th) * (
            1.0 + (3.0 * GELU_A) * sq
        )
        y = tokens_ref[t : t + 32, :].astype(F32) + x * half
        total = total + (y[0:8] + y[8:16]) + (y[16:24] + y[24:32])
    emb = jnp.sum(total, axis=0, keepdims=True) * (1.0 / LEN)
    emb_ref[...] = jnp.broadcast_to(emb, (8, HALF))
    for c in range(COLS):
        block = jnp.broadcast_to(emb[:, c * LANES : (c + 1) * LANES], (N_DP, LANES))
        stage[pl.ds(c, N_DP, stride=SLOT), :] = block
    stage[pl.ds(COLS, N_DP, stride=SLOT), :] = table_ref[...]
    stage[pl.ds(COLS + 1, N_DP, stride=SLOT), :] = jnp.zeros((N_DP, LANES), F32)
    send_ref[...] = stage[...].astype(BF16)


def dots_body(recv_ref, bank_ref, emb_ref, pos_ref, packet_ref, first_ref, count_ref, stage):
    stage[...] = recv_ref[...].astype(F32)
    for c in range(COLS):
        first_ref[:, c * LANES : (c + 1) * LANES] = stage[pl.ds(c, N_DP, stride=SLOT), :]
    count_ref[...] = stage[pl.ds(COLS, N_DP, stride=SLOT), :]
    e = first_ref[...]
    key = bank_ref[...].astype(F32)
    packet_ref[0:OWN, :] = dot(bank_ref[...], e.astype(BF16), NT)
    ones = jnp.ones((8, HALF), F32)
    packet_ref[OWN : OWN + 8, :] = dot(ones, e * e, NT, PRECISE)
    ksq = jnp.sum(key * key, axis=1, keepdims=True)
    packet_ref[OWN + 8 : 2 * OWN + 8, :] = jnp.broadcast_to(ksq, (OWN, LANES))
    emb = emb_ref[0:1, :]
    pos = pos_ref[...].astype(F32)
    rows = (emb * emb, emb * pos, pos * pos)
    for i in range(3):
        value = jnp.sum(rows[i], axis=1, keepdims=True)
        packet_ref[2 * OWN + 8 + 8 * i : 2 * OWN + 16 + 8 * i, :] = jnp.broadcast_to(
            value, (8, LANES)
        )


PACKET = 2 * OWN + 32


def scores_body(
    place, mine_ref, theirs_ref, count_ref, bank_ref, send_ref, coef_ref, kcoef_ref, scal_ref, stage
):
    full = mine_ref[...] + theirs_ref[...]
    en = jnp.sqrt(full[OWN : OWN + 1] + EPSILON)
    kn = jnp.sqrt(full[OWN + 8 : 2 * OWN + 8] + EPSILON)
    scal_ref[...] = full[2 * OWN + 8 : PACKET]
    score = full[0:OWN] / (TEMPER * en * kn)
    count = count_ref[...].T
    row = lax.broadcasted_iota(jnp.int32, (OWN, LANES), 0)
    lane = lax.broadcasted_iota(jnp.int32, (OWN, LANES), 1)
    spread = (row // ROWS == lane).astype(F32)
    count = dot(spread.astype(BF16), count.astype(BF16), NN)
    count = count + (lane == place[1]).astype(F32)
    ec = count * jnp.exp(score)
    z = jnp.sum(ec, axis=0, keepdims=True)
    s = jnp.sum(ec * score, axis=0, keepdims=True)
    blend = ec / kn
    coef_ref[...] = (SCALE / TEMPER) * blend / en
    kcoef_ref[...] = SCALE * ec * score / (kn * kn)
    sums = dot(blend.T, bank_ref[...].astype(F32), NN, PRECISE)
    for c in range(COLS):
        stage[pl.ds(c, N_DP, stride=SLOT), :] = sums[:, c * LANES : (c + 1) * LANES]
    zs = jnp.zeros((OWN, LANES), F32)
    for i, value in enumerate((z, s)):
        upper = value.astype(BF16).astype(F32)
        zs = jnp.where(row == 2 * i, jnp.broadcast_to(upper, (OWN, LANES)), zs)
        zs = jnp.where(row == 2 * i + 1, jnp.broadcast_to(value - upper, (OWN, LANES)), zs)
    stage[pl.ds(COLS, N_DP, stride=SLOT), :] = zs.T
    stage[pl.ds(COLS + 1, N_DP, stride=SLOT), :] = jnp.zeros((N_DP, LANES), F32)
    send_ref[...] = stage[...].astype(BF16)


def grad_body(place, recv_ref, emb_ref, pos_ref, scal_ref, slope_ref, mixed_ref, z_ref):
    acc = jnp.zeros((2 * SLOT, LANES), F32)
    for i in range(0, N_DP * SLOT, 2 * SLOT):
        acc = acc + recv_ref[i : i + 2 * SLOT, :].astype(F32)
    acc = acc[0:SLOT] + acc[SLOT : 2 * SLOT]
    total = jnp.concatenate([acc[c : c + 1] for c in range(COLS)], axis=1)
    tail = acc[COLS : COLS + 1]
    esq = scal_ref[0:1, 0:1]
    inner = scal_ref[8:9, 0:1]
    psq = scal_ref[16:17, 0:1]
    en = jnp.sqrt(esq + EPSILON)
    pn = jnp.sqrt(psq + EPSILON)
    score = inner / (TEMPER * en * pn)
    hit = jnp.exp(score)
    z = tail[:, 0:1] + tail[:, 1:2] + hit
    s = tail[:, 2:3] + tail[:, 3:4] + hit * score
    row_weight = SCALE * (s / z - score)
    unit = emb_ref[0:1, :] / en
    pos = pos_ref[...].astype(F32)
    direction = (SCALE / TEMPER) * (total / z + ((hit / z - 1.0) / pn) * pos)
    grad = (direction - row_weight * unit) / en * (1.0 / LEN)
    for t in range(0, LEN, 32):
        mixed_ref[t : t + 32, :] = (slope_ref[t : t + 32, :] * grad).astype(BF16)
    upper = z.astype(BF16).astype(F32)
    lane = lax.broadcasted_iota(jnp.int32, (8, HALF), 1)
    line = jnp.where(lane == place[1], jnp.broadcast_to(upper, (8, HALF)), 0.0)
    z_ref[...] = jnp.where(lane == place[1] + LANES, jnp.broadcast_to(z - upper, (8, HALF)), line)


def mine_body(place, mine_ref, hidden_ref, w_ref, product_ref, part_ref):
    g = place[0]
    first = pl.multiple_of(g * HALF, HALF)
    part_ref[...] = dot(mine_ref[...], w_ref[pl.ds(first, HALF), :], NN)
    product_ref[...] = dot(mine_ref[...], hidden_ref[...], TN)


def weight_body(
    place, theirs_ref, hidden_ref, w_ref, tokens_ref, z_ref, part_ref, mine_ref, send_ref, pad, small
):
    fill_padded(tokens_ref, pad)
    g = place[0]
    second = pl.multiple_of((1 - g) * HALF, HALF)
    hidden_grad = part_ref[...] + dot(theirs_ref[...], w_ref[pl.ds(second, HALF), :], NN)
    for k in range(KW):
        small[k : k + 1, :] = jnp.sum(
            hidden_grad * pad[5 + k : 5 + k + LEN, :], axis=0, keepdims=True
        )
    small[KW : KW + 1, :] = z_ref[0:1, :]
    extra = small[...]
    product = dot(theirs_ref[...], hidden_ref[...], TN)
    per = PLANE // 2
    for p in range(per):
        span = slice(p * Z_ROWS, (p + 1) * Z_ROWS)
        for side, rows in ((g, mine_ref[span, :]), (1 - g, product[span, :])):
            send_ref[side * per + p] = jnp.concatenate([rows, extra], axis=0).astype(BF16)


BLOCK = OUT_ROWS + 8


def plane_body(recv_ref, send_ref, total, stage):
    for c in range(COLS):
        cols = slice(c * LANES, (c + 1) * LANES)
        acc = recv_ref[0, :, cols].astype(F32)
        for p in range(1, PLANE):
            acc = acc + recv_ref[p, :, cols].astype(F32)
        total[:, cols] = acc
    for c in range(COLS):
        cols = slice(c * LANES, (c + 1) * LANES)
        for z in range(NZ):
            stage[z, c * BLOCK : c * BLOCK + OUT_ROWS, :] = total[
                z * OUT_ROWS : (z + 1) * OUT_ROWS, cols
            ]
            stage[z, c * BLOCK + OUT_ROWS : (c + 1) * BLOCK, :] = total[
                Z_ROWS : Z_ROWS + PACK, cols
            ]
    send_ref[...] = stage[...].astype(BF16)


def final_body(
    recv_ref, coef_ref, kcoef_ref, first_ref, bank_ref, bank_out, kernel_out, weight_out, total
):
    acc = recv_ref[0].astype(F32)
    for z in range(1, NZ):
        acc = acc + recv_ref[z].astype(F32)
    total[...] = acc
    for c in range(COLS):
        cols = slice(c * LANES, (c + 1) * LANES)
        base = c * BLOCK
        weight_out[:, cols] = total[base : base + OUT_ROWS, :] * (1.0 / N_DP)
        kernel_out[:, cols] = total[base + OUT_ROWS : base + OUT_ROWS + KW, :] * (1.0 / N_DP)
    inverse = 1.0 / (total[BLOCK - 1 : BLOCK, :] + total[2 * BLOCK - 1 : 2 * BLOCK, :])
    coef = coef_ref[...] * inverse
    scale = jnp.sum(kcoef_ref[...] * inverse, axis=1, keepdims=True)
    product = dot(coef, first_ref[...], NN, PRECISE)
    bank_out[...] = product - scale * bank_ref[...].astype(F32)


def exchange(value, groups=None):
    return lax.all_to_all(
        value, DP, split_axis=0, concat_axis=0, tiled=True, axis_index_groups=groups
    )


def exchange_slots(value):
    return exchange(value.reshape(N_DP, SLOT, LANES)).reshape(N_DP * SLOT, LANES)


def per_device(tokens_in, dw_kernel, point_weight, positive_emb, bank, neg_owner, neg_block):
    tokens = tokens_in.reshape(LEN, HALF)
    g = lax.axis_index("group")
    d = lax.axis_index(DP)
    place = jnp.stack([g, d]).astype(jnp.int32)
    pad = pltpu.VMEM((LEN + 16, HALF), F32)
    stage = pltpu.VMEM((N_DP * SLOT, LANES), F32)
    flops = 2 * LEN * HALF * HALF

    hidden, other = call(
        conv_body,
        [((LEN, HALF), BF16), ((LEN, HALF), F32)],
        "convolution_and_other_half",
        [pad, pltpu.VMEM((HALF, HALF), BF16), pltpu.SemaphoreType.DMA],
        scalars=1,
        in_hbm=1,
        n_in=2,
        flops=flops,
        limit=62 * 2**20,
    )(place, point_weight, tokens, dw_kernel)
    theirs = lax.ppermute(other, "group", SWAP)
    own, table = call(
        own_body,
        [((LEN, HALF), F32), ((N_DP, LANES), F32)],
        "own_half_and_requests",
        scalars=1,
        n_in=4,
        flops=flops,
    )(place, hidden, point_weight, neg_owner, neg_block.reshape(1, OWN))
    slope, emb, send = call(
        embed_body,
        [((LEN, HALF), F32), ((8, HALF), F32), ((N_DP * SLOT, LANES), BF16)],
        "embedding",
        [stage],
        n_in=4,
    )(own, theirs, tokens, table)
    gathered = exchange_slots(send)
    packet, first, count = call(
        dots_body,
        [((PACKET, LANES), F32), ((N_DP, HALF), F32), ((N_DP, LANES), F32)],
        "inner_products",
        [stage],
        n_in=4,
    )(gathered, bank, emb, positive_emb)
    packet_theirs = lax.ppermute(packet, "group", SWAP)
    send, coef, kcoef, scal = call(
        scores_body,
        [
            ((N_DP * SLOT, LANES), BF16),
            ((OWN, LANES), F32),
            ((OWN, LANES), F32),
            ((24, LANES), F32),
        ],
        "scores",
        [stage],
        scalars=1,
        n_in=4,
    )(place, packet, packet_theirs, count, bank)
    sums = exchange_slots(send)
    mixed, z = call(
        grad_body,
        [((LEN, HALF), BF16), ((8, HALF), F32)],
        "mixed_gradient",
        scalars=1,
        n_in=5,
    )(place, sums, emb, positive_emb, scal, slope)
    mixed_theirs = lax.ppermute(mixed, "group", SWAP)
    product, part = call(
        mine_body,
        [((HALF, HALF), F32), ((LEN, HALF), F32)],
        "weight_gradient_own_half",
        scalars=1,
        n_in=3,
        flops=2 * flops,
    )(place, mixed, hidden, point_weight)
    (send,) = call(
        weight_body,
        [((PLANE, Z_ROWS + PACK, HALF), BF16)],
        "weight_gradient",
        [pad, pltpu.VMEM((8, HALF), F32)],
        scalars=1,
        n_in=7,
        flops=2 * flops,
    )(place, mixed_theirs, hidden, point_weight, tokens, z, part, product)
    planes = exchange(send, PLANES)
    (send,) = call(
        plane_body,
        [((NZ, COLS * BLOCK, LANES), BF16)],
        "sum_over_plane",
        [pltpu.VMEM((Z_ROWS + PACK, HALF), F32), pltpu.VMEM((NZ, COLS * BLOCK, LANES), F32)],
        n_in=1,
    )(planes)
    lines = exchange(send, LINES)
    return tuple(
        call(
            final_body,
            [((OWN, HALF), F32), ((KW, HALF), F32), ((OUT_ROWS, HALF), F32)],
            "outputs",
            [pltpu.VMEM((COLS * BLOCK, LANES), F32)],
            n_in=5,
        )(lines, coef, kcoef, first, bank)
    )


def solution(mesh):
    in_specs = (
        P(DP, None, "group"),
        P(None, "group"),
        P(None, "group"),
        P(DP, "group"),
        P(DP, "group"),
        P(DP, None),
        P(DP),
    )
    out_specs = (P(DP, "group"), P(None, "group"), P(DP, "group"))
    return jax.shard_map(
        per_device, mesh=mesh, in_specs=in_specs, out_specs=out_specs, check_vma=False
    )
```

```python
import jax
import jax.numpy as jnp
from jax import lax
from jax.experimental import pallas as pl
from jax.experimental.pallas import tpu as pltpu
from jax.sharding import PartitionSpec as P

KW = 7
LEN = 256
HALF = 768
N_DP = 128
NX, NY, NZ = 4, 4, 8
PLANE = NX * NY
ROWS = 8
OWN = 128
OUT_ROWS = 12
Z_ROWS = OUT_ROWS * NZ
PACK = 8
SLOT = 8
LANES = 128
COLS = HALF // LANES

TEMPER = 0.07
SCALE = 256.0
EPSILON = 1e-06
GELU_C = 0.7978845608028654
GELU_A = 0.044715
PRECISE = lax.Precision.HIGHEST
F32 = jnp.float32
BF16 = jnp.bfloat16

DP = "dp"
PLANES = [[(x * NY + y) * NZ + z for x in range(NX) for y in range(NY)] for z in range(NZ)]
LINES = [[p * NZ + z for z in range(NZ)] for p in range(PLANE)]
SWAP = [(0, 1), (1, 0)]
VMEM_BYTES = 20 * 2**20

NT = (((1,), (1,)), ((), ()))
NN = (((1,), (0,)), ((), ()))
TN = (((0,), (0,)), ((), ()))


def dot(a, b, dims, precision=None):
    return lax.dot_general(a, b, dims, precision=precision, preferred_element_type=F32)


def call(body, outs, name, scratch=(), scalars=0, n_in=0, flops=0, moved=1 << 20, in_hbm=0, limit=VMEM_BYTES):
    smem = [pl.BlockSpec(memory_space=pltpu.SMEM)] * scalars
    vmem = [pl.BlockSpec(memory_space=pltpu.VMEM)] * n_in
    return pl.pallas_call(
        body,
        out_shape=[jax.ShapeDtypeStruct(s, d) for s, d in outs],
        in_specs=smem + [pl.BlockSpec(memory_space=pl.ANY)] * in_hbm + vmem,
        out_specs=[pl.BlockSpec(memory_space=pltpu.VMEM)] * len(outs),
        scratch_shapes=list(scratch),
        compiler_params=pltpu.CompilerParams(vmem_limit_bytes=limit),
        cost_estimate=pl.CostEstimate(flops=flops, bytes_accessed=moved, transcendentals=0),
        name=name,
    )


def fill_padded(tokens_ref, pad):
    pad[0:8, :] = jnp.zeros((8, HALF), F32)
    pad[LEN + 8 : LEN + 16, :] = jnp.zeros((8, HALF), F32)
    for t in range(0, LEN, 32):
        pad[8 + t : 40 + t, :] = tokens_ref[t : t + 32, :].astype(F32)


def conv_body(
    place, w_hbm, tokens_ref, dw_ref, hidden_ref, other_ref, own_ref, pad, w_ref, sems
):
    copies = []
    for i, side in enumerate((1 - place[0], place[0])):
        start = pl.multiple_of(side * HALF, HALF)
        copies.append(
            pltpu.make_async_copy(w_hbm.at[pl.ds(start, HALF), :], w_ref.at[i], sems.at[i])
        )
        copies[i].start()
    fill_padded(tokens_ref, pad)
    for t in range(0, LEN, 32):
        total = jnp.zeros((32, HALF), F32)
        for k in range(KW):
            total = total + dw_ref[k : k + 1, :] * pad[5 + k + t : 37 + k + t, :]
        hidden_ref[t : t + 32, :] = total.astype(BF16)
    for i, out in enumerate((other_ref, own_ref)):
        copies[i].wait()
        out[...] = dot(hidden_ref[...], w_ref[i], NT)


def table_body(owner_ref, block_ref, table_ref):
    lane = lax.broadcasted_iota(jnp.int32, (OWN, LANES), 1)
    named = (owner_ref[...] == lane).astype(F32)
    blocks = jnp.broadcast_to(block_ref[...].astype(F32), (LANES, OWN)).T
    wanted = (blocks == lane.astype(F32)).astype(F32)
    table_ref[...] = dot(named.T.astype(BF16), wanted.astype(BF16), NN)


def embed_body(own_ref, other_ref, tokens_ref, table_ref, slope_ref, emb_ref, send_ref, stage):
    total = jnp.zeros((8, HALF), F32)
    for t in range(0, LEN, 32):
        x = own_ref[t : t + 32, :] + other_ref[t : t + 32, :]
        sq = x * x
        th = jnp.tanh(GELU_C * x * (1.0 + GELU_A * sq))
        half = 0.5 * (1.0 + th)
        slope_ref[t : t + 32, :] = half + (0.5 * GELU_C) * x * (1.0 - th * th) * (
            1.0 + (3.0 * GELU_A) * sq
        )
        y = tokens_ref[t : t + 32, :].astype(F32) + x * half
        total = total + (y[0:8] + y[8:16]) + (y[16:24] + y[24:32])
    emb = jnp.sum(total, axis=0, keepdims=True) * (1.0 / LEN)
    emb_ref[...] = jnp.broadcast_to(emb, (8, HALF))
    for c in range(COLS):
        block = jnp.broadcast_to(emb[:, c * LANES : (c + 1) * LANES], (N_DP, LANES))
        stage[pl.ds(c, N_DP, stride=SLOT), :] = block
    stage[pl.ds(COLS, N_DP, stride=SLOT), :] = table_ref[...]
    stage[pl.ds(COLS + 1, N_DP, stride=SLOT), :] = jnp.zeros((N_DP, LANES), F32)
    send_ref[...] = stage[...].astype(BF16)


def dots_body(recv_ref, bank_ref, emb_ref, pos_ref, packet_ref, first_ref, count_ref, stage):
    stage[...] = recv_ref[...].astype(F32)
    for c in range(COLS):
        first_ref[:, c * LANES : (c + 1) * LANES] = stage[pl.ds(c, N_DP, stride=SLOT), :]
    count_ref[...] = stage[pl.ds(COLS, N_DP, stride=SLOT), :]
    e = first_ref[...]
    key = bank_ref[...].astype(F32)
    packet_ref[0:OWN, :] = dot(bank_ref[...], e.astype(BF16), NT)
    ones = jnp.ones((8, HALF), F32)
    packet_ref[OWN : OWN + 8, :] = dot(ones, e * e, NT, PRECISE)
    ksq = jnp.sum(key * key, axis=1, keepdims=True)
    packet_ref[OWN + 8 : 2 * OWN + 8, :] = jnp.broadcast_to(ksq, (OWN, LANES))
    emb = emb_ref[0:1, :]
    pos = pos_ref[...].astype(F32)
    rows = (emb * emb, emb * pos, pos * pos)
    for i in range(3):
        value = jnp.sum(rows[i], axis=1, keepdims=True)
        packet_ref[2 * OWN + 8 + 8 * i : 2 * OWN + 16 + 8 * i, :] = jnp.broadcast_to(
            value, (8, LANES)
        )


PACKET = 2 * OWN + 32


def scores_body(
    place, mine_ref, theirs_ref, count_ref, bank_ref, send_ref, coef_ref, kcoef_ref, scal_ref, stage
):
    full = mine_ref[...] + theirs_ref[...]
    en = jnp.sqrt(full[OWN : OWN + 1] + EPSILON)
    kn = jnp.sqrt(full[OWN + 8 : 2 * OWN + 8] + EPSILON)
    scal_ref[...] = full[2 * OWN + 8 : PACKET]
    score = full[0:OWN] / (TEMPER * en * kn)
    count = count_ref[...].T
    row = lax.broadcasted_iota(jnp.int32, (OWN, LANES), 0)
    lane = lax.broadcasted_iota(jnp.int32, (OWN, LANES), 1)
    spread = (row // ROWS == lane).astype(F32)
    count = dot(spread.astype(BF16), count.astype(BF16), NN)
    count = count + (lane == place[1]).astype(F32)
    ec = count * jnp.exp(score)
    z = jnp.sum(ec, axis=0, keepdims=True)
    s = jnp.sum(ec * score, axis=0, keepdims=True)
    blend = ec / kn
    coef_ref[...] = (SCALE / TEMPER) * blend / en
    kcoef_ref[...] = SCALE * ec * score / (kn * kn)
    sums = dot(blend.T, bank_ref[...].astype(F32), NN, PRECISE)
    for c in range(COLS):
        stage[pl.ds(c, N_DP, stride=SLOT), :] = sums[:, c * LANES : (c + 1) * LANES]
    zs = jnp.zeros((OWN, LANES), F32)
    for i, value in enumerate((z, s)):
        upper = value.astype(BF16).astype(F32)
        zs = jnp.where(row == 2 * i, jnp.broadcast_to(upper, (OWN, LANES)), zs)
        zs = jnp.where(row == 2 * i + 1, jnp.broadcast_to(value - upper, (OWN, LANES)), zs)
    stage[pl.ds(COLS, N_DP, stride=SLOT), :] = zs.T
    stage[pl.ds(COLS + 1, N_DP, stride=SLOT), :] = jnp.zeros((N_DP, LANES), F32)
    send_ref[...] = stage[...].astype(BF16)


def grad_body(place, recv_ref, emb_ref, pos_ref, scal_ref, slope_ref, mixed_ref, z_ref):
    acc = jnp.zeros((2 * SLOT, LANES), F32)
    for i in range(0, N_DP * SLOT, 2 * SLOT):
        acc = acc + recv_ref[i : i + 2 * SLOT, :].astype(F32)
    acc = acc[0:SLOT] + acc[SLOT : 2 * SLOT]
    total = jnp.concatenate([acc[c : c + 1] for c in range(COLS)], axis=1)
    tail = acc[COLS : COLS + 1]
    esq = scal_ref[0:1, 0:1]
    inner = scal_ref[8:9, 0:1]
    psq = scal_ref[16:17, 0:1]
    en = jnp.sqrt(esq + EPSILON)
    pn = jnp.sqrt(psq + EPSILON)
    score = inner / (TEMPER * en * pn)
    hit = jnp.exp(score)
    z = tail[:, 0:1] + tail[:, 1:2] + hit
    s = tail[:, 2:3] + tail[:, 3:4] + hit * score
    row_weight = SCALE * (s / z - score)
    unit = emb_ref[0:1, :] / en
    pos = pos_ref[...].astype(F32)
    direction = (SCALE / TEMPER) * (total / z + ((hit / z - 1.0) / pn) * pos)
    grad = (direction - row_weight * unit) / en * (1.0 / LEN)
    for t in range(0, LEN, 32):
        mixed_ref[t : t + 32, :] = (slope_ref[t : t + 32, :] * grad).astype(BF16)
    upper = z.astype(BF16).astype(F32)
    lane = lax.broadcasted_iota(jnp.int32, (8, HALF), 1)
    line = jnp.where(lane == place[1], jnp.broadcast_to(upper, (8, HALF)), 0.0)
    z_ref[...] = jnp.where(lane == place[1] + LANES, jnp.broadcast_to(z - upper, (8, HALF)), line)


def mine_body(place, mine_ref, hidden_ref, w_ref, product_ref, part_ref):
    g = place[0]
    first = pl.multiple_of(g * HALF, HALF)
    part_ref[...] = dot(mine_ref[...], w_ref[pl.ds(first, HALF), :], NN)
    product_ref[...] = dot(mine_ref[...], hidden_ref[...], TN)


def weight_body(
    place, theirs_ref, hidden_ref, w_ref, tokens_ref, z_ref, part_ref, mine_ref, send_ref, pad, small
):
    fill_padded(tokens_ref, pad)
    g = place[0]
    second = pl.multiple_of((1 - g) * HALF, HALF)
    hidden_grad = part_ref[...] + dot(theirs_ref[...], w_ref[pl.ds(second, HALF), :], NN)
    for k in range(KW):
        small[k : k + 1, :] = jnp.sum(
            hidden_grad * pad[5 + k : 5 + k + LEN, :], axis=0, keepdims=True
        )
    small[KW : KW + 1, :] = z_ref[0:1, :]
    extra = small[...]
    product = dot(theirs_ref[...], hidden_ref[...], TN)
    per = PLANE // 2
    for p in range(per):
        span = slice(p * Z_ROWS, (p + 1) * Z_ROWS)
        for side, rows in ((g, mine_ref[span, :]), (1 - g, product[span, :])):
            send_ref[side * per + p] = jnp.concatenate([rows, extra], axis=0).astype(BF16)


BLOCK = OUT_ROWS + 8


def plane_body(recv_ref, send_ref, total, stage):
    for c in range(COLS):
        cols = slice(c * LANES, (c + 1) * LANES)
        acc = recv_ref[0, :, cols].astype(F32)
        for p in range(1, PLANE):
            acc = acc + recv_ref[p, :, cols].astype(F32)
        total[:, cols] = acc
    for c in range(COLS):
        cols = slice(c * LANES, (c + 1) * LANES)
        for z in range(NZ):
            stage[z, c * BLOCK : c * BLOCK + OUT_ROWS, :] = total[
                z * OUT_ROWS : (z + 1) * OUT_ROWS, cols
            ]
            stage[z, c * BLOCK + OUT_ROWS : (c + 1) * BLOCK, :] = total[
                Z_ROWS : Z_ROWS + PACK, cols
            ]
    send_ref[...] = stage[...].astype(BF16)


def final_body(
    recv_ref, coef_ref, kcoef_ref, first_ref, bank_ref, bank_out, kernel_out, weight_out, total
):
    acc = recv_ref[0].astype(F32)
    for z in range(1, NZ):
        acc = acc + recv_ref[z].astype(F32)
    total[...] = acc
    for c in range(COLS):
        cols = slice(c * LANES, (c + 1) * LANES)
        base = c * BLOCK
        weight_out[:, cols] = total[base : base + OUT_ROWS, :] * (1.0 / N_DP)
        kernel_out[:, cols] = total[base + OUT_ROWS : base + OUT_ROWS + KW, :] * (1.0 / N_DP)
    inverse = 1.0 / (total[BLOCK - 1 : BLOCK, :] + total[2 * BLOCK - 1 : 2 * BLOCK, :])
    coef = coef_ref[...] * inverse
    scale = jnp.sum(kcoef_ref[...] * inverse, axis=1, keepdims=True)
    product = dot(coef, first_ref[...], NN, PRECISE)
    bank_out[...] = product - scale * bank_ref[...].astype(F32)


def exchange(value, groups=None):
    return lax.all_to_all(
        value, DP, split_axis=0, concat_axis=0, tiled=True, axis_index_groups=groups
    )


def exchange_slots(value):
    return exchange(value.reshape(N_DP, SLOT, LANES)).reshape(N_DP * SLOT, LANES)


def per_device(tokens_in, dw_kernel, point_weight, positive_emb, bank, neg_owner, neg_block):
    tokens = tokens_in.reshape(LEN, HALF)
    g = lax.axis_index("group")
    d = lax.axis_index(DP)
    place = jnp.stack([g, d]).astype(jnp.int32)
    pad = pltpu.VMEM((LEN + 16, HALF), F32)
    stage = pltpu.VMEM((N_DP * SLOT, LANES), F32)
    flops = 2 * LEN * HALF * HALF

    hidden, other, own = call(
        conv_body,
        [((LEN, HALF), BF16), ((LEN, HALF), F32), ((LEN, HALF), F32)],
        "convolution_and_product",
        [pad, pltpu.VMEM((2, HALF, HALF), BF16), pltpu.SemaphoreType.DMA((2,))],
        scalars=1,
        in_hbm=1,
        n_in=2,
        flops=flops,
        limit=62 * 2**20,
    )(place, point_weight, tokens, dw_kernel)
    theirs = lax.ppermute(other, "group", SWAP)
    (table,) = call(table_body, [((N_DP, LANES), F32)], "requests", n_in=2)(
        neg_owner, neg_block.reshape(1, OWN)
    )
    slope, emb, send = call(
        embed_body,
        [((LEN, HALF), F32), ((8, HALF), F32), ((N_DP * SLOT, LANES), BF16)],
        "embedding",
        [stage],
        n_in=4,
    )(own, theirs, tokens, table)
    gathered = exchange_slots(send)
    packet, first, count = call(
        dots_body,
        [((PACKET, LANES), F32), ((N_DP, HALF), F32), ((N_DP, LANES), F32)],
        "inner_products",
        [stage],
        n_in=4,
    )(gathered, bank, emb, positive_emb)
    packet_theirs = lax.ppermute(packet, "group", SWAP)
    send, coef, kcoef, scal = call(
        scores_body,
        [
            ((N_DP * SLOT, LANES), BF16),
            ((OWN, LANES), F32),
            ((OWN, LANES), F32),
            ((24, LANES), F32),
        ],
        "scores",
        [stage],
        scalars=1,
        n_in=4,
    )(place, packet, packet_theirs, count, bank)
    sums = exchange_slots(send)
    mixed, z = call(
        grad_body,
        [((LEN, HALF), BF16), ((8, HALF), F32)],
        "mixed_gradient",
        scalars=1,
        n_in=5,
    )(place, sums, emb, positive_emb, scal, slope)
    mixed_theirs = lax.ppermute(mixed, "group", SWAP)
    product, part = call(
        mine_body,
        [((HALF, HALF), F32), ((LEN, HALF), F32)],
        "weight_gradient_own_half",
        scalars=1,
        n_in=3,
        flops=2 * flops,
    )(place, mixed, hidden, point_weight)
    (send,) = call(
        weight_body,
        [((PLANE, Z_ROWS + PACK, HALF), BF16)],
        "weight_gradient",
        [pad, pltpu.VMEM((8, HALF), F32)],
        scalars=1,
        n_in=7,
        flops=2 * flops,
    )(place, mixed_theirs, hidden, point_weight, tokens, z, part, product)
    planes = exchange(send, PLANES)
    (send,) = call(
        plane_body,
        [((NZ, COLS * BLOCK, LANES), BF16)],
        "sum_over_plane",
        [pltpu.VMEM((Z_ROWS + PACK, HALF), F32), pltpu.VMEM((NZ, COLS * BLOCK, LANES), F32)],
        n_in=1,
    )(planes)
    lines = exchange(send, LINES)
    return tuple(
        call(
            final_body,
            [((OWN, HALF), F32), ((KW, HALF), F32), ((OUT_ROWS, HALF), F32)],
            "outputs",
            [pltpu.VMEM((COLS * BLOCK, LANES), F32)],
            n_in=5,
        )(lines, coef, kcoef, first, bank)
    )


def solution(mesh):
    in_specs = (
        P(DP, None, "group"),
        P(None, "group"),
        P(None, "group"),
        P(DP, "group"),
        P(DP, "group"),
        P(DP, None),
        P(DP),
    )
    out_specs = (P(DP, "group"), P(None, "group"), P(DP, "group"))
    return jax.shard_map(
        per_device, mesh=mesh, in_specs=in_specs, out_specs=out_specs, check_vma=False
    )
```
